32 devices in a mesh: groups: 2 (over y), slab: 8 (over z, x), cross: 2 (over core).
Axes of the slice: x: 2, y: 2, z: 4, core: 2. Of those that a mesh axis runs over, the one named last changes fastest.
Arguments:
- basis: bfloat16 [1024, 64, 512], P(('groups', 'slab', 'cross')), parts along dimension 0, may hold values from -0.1796875 to 0.1796875
- stiff: bfloat16 [1024, 128, 128], P(('groups', 'slab', 'cross')), parts along dimension 0, may hold values from -0.5 to 0.5
- soft: bfloat16 [1024, 64, 64], P(('groups', 'slab', 'cross')), parts along dimension 0, may hold values from -9 to 9
- under: int32 [1024], P(('groups', 'slab', 'cross')), parts along dimension 0, may hold values 0 or 1
Outputs:
- k_reduced: float32 [1024, 512], P(('groups', 'slab', 'cross')), parts along dimension 0
- electrode_reduced: float32 [4096, 512], P(('groups', 'slab', 'cross')), parts along dimension 0
The draws below stay inside these ranges and needn't reach their ends.
There are 2 independent parts, one for each index of `groups`. The reference program is written for one: setup_inputs(seed, part) draws one part's arguments, and reference() takes and returns one part's arrays. A program takes and returns all parts, laid end to end along the dimension named above; each array names one. Nothing has to cross between parts.
All inputs are finite; a program needn't handle non-finite values. No bound on the sum of `under` on one device may be relied on, other than what follows from the above.
Results may differ from the reference program's by a relative error of at most 0.0029.
Values may be sent and summed in bfloat16 or wider, within the bound.
A program may use at most 64 MiB of HBM per device.

```python
import jax
import jax.numpy as jnp
from jax import lax

NB = 64
R = 512
CELLS = 32
ELEC = 4
NCELL = 512


def with_ends(result, stream_key, least, largest):
    place = [jax.random.randint(jax.random.fold_in(stream_key, axis), (), 0, length) for axis, length in enumerate(result.shape)]
    longest = result.shape.index(max(result.shape))
    neighbour = place[:longest] + [(place[longest] + 1) % result.shape[longest]] + place[longest + 1:]
    return result.at[tuple(place)].set(least).at[tuple(neighbour)].set(largest)


def steps_of(rng, shape, shards, least, high):
    loudness = 1.0
    for position, shards_of in shards:
        draws = jax.random.uniform(jax.random.fold_in(jax.random.fold_in(rng, 6), position), (shards_of,), jnp.float32, least / len(shards), high / len(shards))
        loudness = loudness * jnp.repeat(jnp.exp(draws), shape[position] // shards_of).reshape((-1,) + (1,) * (len(shape) - 1 - position))
    return loudness


def bell_draw(key, dims, deviation, bound, pieces=(), kind=jnp.bfloat16):
    entries = jax.random.normal(key, dims, jnp.float32) * deviation
    if len(pieces) > 0:
        entries = steps_of(key, dims, pieces, -0.22, 0.18) * entries
    return jnp.clip(entries, min=-bound, max=bound).astype(kind)


def setup_inputs(seed: int = 0, part: int = 0) -> dict:
    key_of = jax.random.split(jax.random.key(seed), 5)
    part_keys = jax.random.split(jax.random.fold_in(key_of[4], part), 5)
    basis = bell_draw(part_keys[0], (NCELL, NB, R), 0.03, 0.1796875, ((0, 16),))
    stiff = bell_draw(part_keys[1], (NCELL, 2 * NB, 2 * NB), (2 * NB) ** -0.5, 0.5, ((0, 16),))
    soft = bell_draw(part_keys[2], (NCELL, NB, NB), 1.5, 9.0, ((0, 16),))
    under = with_ends((jax.random.randint(part_keys[3], (NCELL,), 0, 4) < 3).astype(jnp.int32), jax.random.fold_in(part_keys[3], 1), 0, 1)
    return {"basis": basis, "stiff": stiff, "soft": soft, "under": under}


def reference(basis, stiff, soft, under):
    width = 4 * CELLS
    zero_cell = jnp.zeros((1, NB, R), jnp.bfloat16)
    padded = jnp.concatenate([zero_cell, basis, zero_cell], axis=0)
    stiff_pad = jnp.concatenate([jnp.zeros((1, 2 * NB, 2 * NB), jnp.bfloat16), stiff], axis=0)

    def block(k_total, index):
        first = (index * width).astype(jnp.int32)
        cells = lax.dynamic_slice_in_dim(padded, first, width + 2, 0)
        blocks = lax.dynamic_slice_in_dim(stiff_pad, first, width + 1, 0)
        pairs = jnp.concatenate([cells[:-1], cells[1:]], axis=1)
        prod = jnp.einsum("cij,cjr->cir", blocks.astype(jnp.float32), pairs.astype(jnp.float32))
        action = prod[1:, :NB] + prod[:-1, NB:]
        stiff_basis = action.astype(jnp.bfloat16).reshape(width * NB, R)
        own = cells[1:-1]
        flat = own.reshape(width * NB, R)
        k_total = k_total + jnp.dot(flat.T, stiff_basis, preferred_element_type=jnp.float32)
        mask = lax.dynamic_slice_in_dim(under, first, width, 0).astype(jnp.float32)
        soft_blk = lax.dynamic_slice_in_dim(soft, first, width, 0).astype(jnp.float32) * mask[:, None, None]
        soft_basis = jnp.einsum("cij,cjr->cir", soft_blk, own.astype(jnp.float32)).astype(jnp.bfloat16)
        elec = jnp.dot(flat.T, soft_basis.reshape(width * NB, R), preferred_element_type=jnp.float32)
        return k_total, elec

    k_reduced, electrode = lax.scan(block, jnp.zeros((R, R), jnp.float32), jnp.arange(ELEC, dtype=jnp.int32))
    return k_reduced, electrode.reshape(ELEC * R, R)
```

```python
import functools

import jax
import jax.numpy as jnp
from jax import lax
from jax.experimental import pallas as pl
from jax.experimental.pallas import tpu as pltpu
from jax.sharding import PartitionSpec as P

MESH = pl.DeviceIdType.MESH
BF16 = jnp.bfloat16
F32 = jnp.float32


def shifted(x, axis, by):
    length = lax.axis_size(axis)
    pairs = [(i, i + by) for i in range(length) if 0 <= i + by < length]
    return lax.ppermute(x, axis, pairs)


def partner(x, axis, bit):
    return lax.ppermute(x, axis, [(i, i ^ 1 << bit) for i in range(lax.axis_size(axis))])


def plain_body(basis, stiff, soft, under):
    cells, layer, width = basis.shape
    nextcell = shifted(basis[:1], ("slab", "cross"), -1)
    upper_cells = jnp.concatenate([basis[1:], nextcell], axis=0)
    pairs = jnp.concatenate([basis, upper_cells], axis=1)
    prod = jnp.einsum("cij,cjr->cir", stiff, pairs, preferred_element_type=jnp.float32)
    carry_in = shifted(prod[-1:, layer:], ("slab", "cross"), 1)
    action = prod[:, :layer] + jnp.concatenate([carry_in, prod[:-1, layer:]], axis=0)
    flat_basis = basis.reshape(cells * layer, width)
    flat_stiff = action.astype(jnp.bfloat16).reshape(cells * layer, width)
    k_reduced = lax.psum_scatter(
        lax.dot_general(
            flat_basis, flat_stiff, (((0,), (0,)), ((), ())), preferred_element_type=jnp.float32
        ),
        ("slab", "cross"),
        scatter_dimension=0,
        tiled=True,
    )
    masked = soft * under.astype(jnp.bfloat16)[:, None, None]
    soft_basis = jnp.einsum("cij,cjr->cir", masked, basis, preferred_element_type=jnp.float32)
    flat_soft = soft_basis.astype(jnp.bfloat16).reshape(cells * layer, width)
    partial_sum = lax.dot_general(
        flat_basis, flat_soft, (((0,), (0,)), ((), ())), preferred_element_type=jnp.float32
    )
    parity = lax.axis_index("slab") % 2
    halves = partial_sum.reshape(2, width // 2, width)
    mine = lax.dynamic_index_in_dim(halves, parity, 0, keepdims=False)
    other = lax.dynamic_index_in_dim(halves, 1 - parity, 0, keepdims=False)
    paired = mine + partner(other, "slab", 0)
    electrode_rows = lax.psum_scatter(paired, "cross", scatter_dimension=0, tiled=True)
    return (k_reduced, electrode_rows)


def fused_kernel(
    nz, cells, layer, width, chunk,
    basis, stiff, soft, under, k_out, e_out,
    ext, turned, stiff_v, stiff_p, soft_v, acted,
    k_own, k_core_s, k_core_r, k_x_s, k_x_r, k_z_s, k_z_r,
    e_own, e_core_s, e_core_r, e_x_s, e_x_r,
    load_sem, halo_s, halo_r, kc_s, kc_r, kx_s, kx_r, kz_s, kz_r, ec_s, ec_r, ex_s, ex_r,
):
    slab = lax.axis_index("slab")
    core = lax.axis_index("cross")
    z, x = slab // 2, slab % 2
    here = slab * 2 + core
    count = nz * 4
    rows = cells * layer
    chunks = width // chunk
    k_rows = width // count
    e_rows = width // 4
    group = 4

    core_peer = {"cross": 1 - core}
    x_peer = {"slab": slab + 1 - 2 * x}
    z_peers = [{"slab": ((z + d) % nz) * 2 + x} for d in range(1, nz)]
    before = (here + count - 1) % count
    after = (here + 1) % count
    before_peer = {"slab": before // 2, "cross": before % 2}
    after_peer = {"slab": after // 2, "cross": after % 2}

    barrier = pltpu.get_barrier_semaphore()
    peers = [core_peer, x_peer, *z_peers, before_peer, after_peer]
    for peer in peers:
        pl.semaphore_signal(barrier, inc=1, device_id=peer, device_id_type=MESH)

    loads = [
        pltpu.make_async_copy(basis, ext.at[pl.ds(layer, rows)], load_sem.at[0]),
        pltpu.make_async_copy(stiff, stiff_v, load_sem.at[1]),
        pltpu.make_async_copy(soft, soft_v, load_sem.at[2]),
    ]
    for load in loads:
        load.start()

    pl.semaphore_wait(barrier, len(peers))

    def remote(src, dst, send, recv, peer):
        return pltpu.make_async_remote_copy(
            src_ref=src, dst_ref=dst, send_sem=send, recv_sem=recv,
            device_id=peer, device_id_type=MESH,
        )

    first_out = remote(
        basis.at[pl.ds(0, layer)], ext.at[pl.ds(layer + rows, layer)],
        halo_s.at[0], halo_r.at[0], before_peer,
    )
    last_out = remote(
        basis.at[pl.ds(rows - layer, layer)], ext.at[pl.ds(0, layer)],
        halo_s.at[1], halo_r.at[1], after_peer,
    )
    lower_out = remote(
        stiff.at[cells - 1, pl.ds(layer, layer)], stiff_p,
        halo_s.at[2], halo_r.at[2], after_peer,
    )

    @pl.when(here > 0)
    def _():
        first_out.start()

    @pl.when(here < count - 1)
    def _():
        last_out.start()
        lower_out.start()

    loads[0].wait()

    def turn(g, _):
        at = pl.multiple_of(g * chunk, chunk)
        turned[:, pl.ds(at, chunk)] = ext[pl.ds(pl.multiple_of(layer + at, layer), chunk), :].T
        return 0

    lax.fori_loop(0, rows // chunk, turn, 0)
    loads[1].wait()
    loads[2].wait()

    @pl.when(here > 0)
    def _():
        last_out.wait_recv()
        lower_out.wait_recv()

    @pl.when(here == 0)
    def _():
        ext[pl.ds(0, layer), :] = jnp.zeros((layer, width), BF16)
        stiff_p[...] = jnp.zeros(stiff_p.shape, BF16)

    @pl.when(here < count - 1)
    def _():
        first_out.wait_recv()

    @pl.when(here == count - 1)
    def _():
        ext[pl.ds(layer + rows, layer), :] = jnp.zeros((layer, width), BF16)

    def stiff_chunk(j):
        cols = pl.ds(j * chunk, chunk)

        def step(g, carry):
            for i in range(group):
                c = g * group + i
                at = pl.multiple_of(c * layer, layer)
                prod = jnp.dot(
                    stiff_v[c],
                    ext[pl.ds(pl.multiple_of(at + layer, layer), 2 * layer), cols],
                    preferred_element_type=F32,
                )
                acted[pl.ds(at, layer), cols] = (prod[:layer] + carry).astype(BF16)
                carry = prod[layer:]
            return carry

        carry = jnp.dot(stiff_p[...], ext[pl.ds(0, 2 * layer), cols], preferred_element_type=F32)
        lax.fori_loop(0, cells // group, step, carry)

    def soft_chunk(j):
        cols = pl.ds(j * chunk, chunk)

        def step(g, _):
            for i in range(group):
                c = g * group + i
                at = pl.multiple_of(c * layer, layer)
                masked = soft_v[c] * under[c].astype(F32).astype(BF16)
                prod = jnp.dot(
                    masked,
                    ext[pl.ds(pl.multiple_of(at + layer, layer), layer), cols],
                    preferred_element_type=F32,
                )
                acted[pl.ds(at, layer), cols] = prod.astype(BF16)
            return 0

        lax.fori_loop(0, cells // group, step, 0)

    def project(j):
        return jnp.dot(
            turned[...], acted[:, pl.ds(j * chunk, chunk)], preferred_element_type=F32
        )

    kc = [remote(k_core_s.at[j, 1 - core], k_core_r.at[j], kc_s.at[j], kc_r.at[j], core_peer)
          for j in range(chunks)]
    kx = [remote(k_x_s.at[j], k_x_r.at[j], kx_s.at[j], kx_r.at[j], x_peer) for j in range(chunks)]
    kz = [[remote(k_z_s.at[j, d], k_z_r.at[j, d], kz_s.at[j, d], kz_r.at[j, d], z_peers[d])
           for d in range(nz - 1)] for j in range(chunks)]
    ec = [remote(e_core_s.at[j, 1 - core], e_core_r.at[j], ec_s.at[j], ec_r.at[j], core_peer)
          for j in range(chunks)]
    ex = [remote(e_x_s.at[j], e_x_r.at[j], ex_s.at[j], ex_r.at[j], x_peer) for j in range(chunks)]

    def k_start(j):
        part = project(j)
        for c in range(2):
            for xx in range(2):
                for zz in range(nz):
                    at = ((zz * 2 + xx) * 2 + c) * k_rows
                    block = part[at:at + k_rows]
                    k_own[j, c, xx, zz] = block
                    k_core_s[j, c, xx, zz] = block.astype(BF16)
        kc[j].start()

    def k_across(j):
        kc[j].wait_recv()
        k_x_s[j] = (k_own[j, core, 1 - x] + k_core_r[j, 1 - x].astype(F32)).astype(BF16)
        kx[j].start()
        k_own[j, core, x] = k_own[j, core, x] + k_core_r[j, x].astype(F32)

    def k_along(j):
        kx[j].wait_recv()
        for d in range(nz - 1):
            to = (z + d + 1) % nz
            k_z_s[j, d] = (k_own[j, core, x, to] + k_x_r[j, to].astype(F32)).astype(BF16)
            kz[j][d].start()

    def k_end(j):
        total = k_own[j, core, x, z] + k_x_r[j, z].astype(F32)
        for d in range(nz - 1):
            kz[j][d].wait_recv()
            total = total + k_z_r[j, d].astype(F32)
        k_out[:, pl.ds(j * chunk, chunk)] = total

    def e_start(j):
        part = project(j)
        for c in range(2):
            for xx in range(2):
                at = (xx * 2 + c) * e_rows
                block = part[at:at + e_rows]
                e_own[j, c, xx] = block
                e_core_s[j, c, xx] = block.astype(BF16)
        ec[j].start()

    def e_across(j):
        ec[j].wait_recv()
        e_x_s[j] = (e_own[j, core, 1 - x] + e_core_r[j, 1 - x].astype(F32)).astype(BF16)
        ex[j].start()

    def e_end(j):
        mine = e_own[j, core, x] + e_core_r[j, x].astype(F32)
        ex[j].wait_recv()
        e_out[:, pl.ds(j * chunk, chunk)] = mine + ex_in(j)

    def ex_in(j):
        return e_x_r[j].astype(F32)

    stiff_chunk(0)
    k_start(0)
    stiff_chunk(1)
    k_across(0)
    k_start(1)
    soft_chunk(0)
    k_across(1)
    k_along(0)
    e_start(0)
    soft_chunk(1)
    e_across(0)
    k_along(1)
    e_start(1)
    k_end(0)
    e_across(1)
    e_end(0)
    k_end(1)
    e_end(1)

    @pl.when(here > 0)
    def _():
        first_out.wait_send()

    @pl.when(here < count - 1)
    def _():
        last_out.wait_send()
        lower_out.wait_send()

    for j in range(chunks):
        kc[j].wait_send()
        kx[j].wait_send()
        for d in range(nz - 1):
            kz[j][d].wait_send()
        ec[j].wait_send()
        ex[j].wait_send()


def fused_body(basis, stiff, soft, under):
    cells, layer, width = basis.shape
    rows = cells * layer
    nz = lax.axis_size("slab") // 2
    chunk = 256
    chunks = width // chunk
    k_rows = width // (4 * nz)
    e_rows = width // 4
    hbm = pl.BlockSpec(memory_space=pl.ANY)
    vmem = pl.BlockSpec(memory_space=pltpu.VMEM)
    dma = pltpu.SemaphoreType.DMA
    return pl.pallas_call(
        functools.partial(fused_kernel, nz, cells, layer, width, chunk),
        out_shape=(
            jax.ShapeDtypeStruct((k_rows, width), F32),
            jax.ShapeDtypeStruct((e_rows, width), F32),
        ),
        in_specs=[hbm, hbm, hbm, pl.BlockSpec(memory_space=pltpu.SMEM)],
        out_specs=(vmem, vmem),
        scratch_shapes=[
            pltpu.VMEM((rows + 2 * layer, width), BF16),
            pltpu.VMEM((width, rows), BF16),
            pltpu.VMEM((cells, 2 * layer, 2 * layer), BF16),
            pltpu.VMEM((layer, 2 * layer), BF16),
            pltpu.VMEM((cells, layer, layer), BF16),
            pltpu.VMEM((rows, width), BF16),
            pltpu.VMEM((chunks, 2, 2, nz, k_rows, chunk), F32),
            pltpu.VMEM((chunks, 2, 2, nz, k_rows, chunk), BF16),
            pltpu.VMEM((chunks, 2, nz, k_rows, chunk), BF16),
            pltpu.VMEM((chunks, nz, k_rows, chunk), BF16),
            pltpu.VMEM((chunks, nz, k_rows, chunk), BF16),
            pltpu.VMEM((chunks, nz - 1, k_rows, chunk), BF16),
            pltpu.VMEM((chunks, nz - 1, k_rows, chunk), BF16),
            pltpu.VMEM((chunks, 2, 2, e_rows, chunk), F32),
            pltpu.VMEM((chunks, 2, 2, e_rows, chunk), BF16),
            pltpu.VMEM((chunks, 2, e_rows, chunk), BF16),
            pltpu.VMEM((chunks, e_rows, chunk), BF16),
            pltpu.VMEM((chunks, e_rows, chunk), BF16),
            dma((3,)), dma((3,)), dma((3,)),
            dma((chunks,)), dma((chunks,)), dma((chunks,)), dma((chunks,)),
            dma((chunks, nz - 1)), dma((chunks, nz - 1)),
            dma((chunks,)), dma((chunks,)), dma((chunks,)), dma((chunks,)),
        ],
        compiler_params=pltpu.CompilerParams(
            collective_id=0, has_side_effects=True, vmem_limit_bytes=48 << 20
        ),
        name="fused",
    )(basis.reshape(rows, width), stiff, soft, under)


def solution(mesh):
    placed = (
        P(("groups", "slab", "cross"), None, None),
        P(("groups", "slab", "cross"), None, None),
        P(("groups", "slab", "cross"), None, None),
        P(("groups", "slab", "cross")),
    )

    def body(basis, stiff, soft, under):
        cells, layer, width = basis.shape
        members = mesh.shape["slab"] * mesh.shape["cross"]
        fits = (
            mesh.shape["cross"] == 2
            and mesh.shape["slab"] % 2 == 0
            and mesh.shape["slab"] >= 4
            and width == 512
            and layer == 64
            and cells % 4 == 0
            and (cells * layer) % 256 == 0
            and width // members >= 16
            and (width // members) % 16 == 0
        )
        return (fused_body if fits else plain_body)(basis, stiff, soft, under)

    return jax.shard_map(
        body,
        mesh=mesh,
        in_specs=placed,
        out_specs=(P(("groups", "slab", "cross"), None), P(("groups", "slab", "cross"), None)),
        check_vma=False,
    )
```

```python
import functools

import jax
import jax.numpy as jnp
from jax import lax
from jax.experimental import pallas as pl
from jax.experimental.pallas import tpu as pltpu
from jax.sharding import PartitionSpec as P

MESH = pl.DeviceIdType.MESH
BF16 = jnp.bfloat16
F32 = jnp.float32


def shifted(x, axis, by):
    length = lax.axis_size(axis)
    pairs = [(i, i + by) for i in range(length) if 0 <= i + by < length]
    return lax.ppermute(x, axis, pairs)


def partner(x, axis, bit):
    return lax.ppermute(x, axis, [(i, i ^ 1 << bit) for i in range(lax.axis_size(axis))])


def plain_body(basis, stiff, soft, under):
    cells, layer, width = basis.shape
    nextcell = shifted(basis[:1], ("slab", "cross"), -1)
    upper_cells = jnp.concatenate([basis[1:], nextcell], axis=0)
    pairs = jnp.concatenate([basis, upper_cells], axis=1)
    prod = jnp.einsum("cij,cjr->cir", stiff, pairs, preferred_element_type=jnp.float32)
    carry_in = shifted(prod[-1:, layer:], ("slab", "cross"), 1)
    action = prod[:, :layer] + jnp.concatenate([carry_in, prod[:-1, layer:]], axis=0)
    flat_basis = basis.reshape(cells * layer, width)
    flat_stiff = action.astype(jnp.bfloat16).reshape(cells * layer, width)
    k_reduced = lax.psum_scatter(
        lax.dot_general(
            flat_basis, flat_stiff, (((0,), (0,)), ((), ())), preferred_element_type=jnp.float32
        ),
        ("slab", "cross"),
        scatter_dimension=0,
        tiled=True,
    )
    masked = soft * under.astype(jnp.bfloat16)[:, None, None]
    soft_basis = jnp.einsum("cij,cjr->cir", masked, basis, preferred_element_type=jnp.float32)
    flat_soft = soft_basis.astype(jnp.bfloat16).reshape(cells * layer, width)
    partial_sum = lax.dot_general(
        flat_basis, flat_soft, (((0,), (0,)), ((), ())), preferred_element_type=jnp.float32
    )
    parity = lax.axis_index("slab") % 2
    halves = partial_sum.reshape(2, width // 2, width)
    mine = lax.dynamic_index_in_dim(halves, parity, 0, keepdims=False)
    other = lax.dynamic_index_in_dim(halves, 1 - parity, 0, keepdims=False)
    paired = mine + partner(other, "slab", 0)
    electrode_rows = lax.psum_scatter(paired, "cross", scatter_dimension=0, tiled=True)
    return (k_reduced, electrode_rows)


def fused_kernel(
    nz, cells, layer, width, chunk,
    basis, stiff, soft, under, k_out, e_out,
    ext, stiff_v, stiff_p, soft_v, mask_v, acted, softened,
    k_own, k_core_s, k_core_r, k_x_s, k_x_r, k_z_s, k_z_r,
    e_own, e_core_s, e_core_r, e_x_s, e_x_r,
    load_sem, halo_s, halo_r, kc_s, kc_r, kx_s, kx_r, kz_s, kz_r, ec_s, ec_r, ex_s, ex_r,
):
    slab = lax.axis_index("slab")
    core = lax.axis_index("cross")
    z, x = slab // 2, slab % 2
    here = slab * 2 + core
    count = nz * 4
    rows = cells * layer
    chunks = width // chunk
    k_rows = width // count
    e_rows = width // 4

    core_peer = {"cross": 1 - core}
    x_peer = {"slab": slab + 1 - 2 * x}
    z_peers = [{"slab": ((z + d) % nz) * 2 + x} for d in range(1, nz)]
    before = (here + count - 1) % count
    after = (here + 1) % count
    before_peer = {"slab": before // 2, "cross": before % 2}
    after_peer = {"slab": after // 2, "cross": after % 2}

    barrier = pltpu.get_barrier_semaphore()
    peers = [core_peer, x_peer, *z_peers, before_peer, after_peer]
    for peer in peers:
        pl.semaphore_signal(barrier, inc=1, device_id=peer, device_id_type=MESH)

    loads = [
        pltpu.make_async_copy(basis, ext.at[pl.ds(layer, rows)], load_sem.at[0]),
        pltpu.make_async_copy(stiff, stiff_v, load_sem.at[1]),
        pltpu.make_async_copy(soft, soft_v, load_sem.at[2]),
        pltpu.make_async_copy(under, mask_v, load_sem.at[3]),
    ]
    for load in loads:
        load.start()

    pl.semaphore_wait(barrier, len(peers))

    def remote(src, dst, send, recv, peer):
        return pltpu.make_async_remote_copy(
            src_ref=src, dst_ref=dst, send_sem=send, recv_sem=recv,
            device_id=peer, device_id_type=MESH,
        )

    first_out = remote(
        basis.at[pl.ds(0, layer)], ext.at[pl.ds(layer + rows, layer)],
        halo_s.at[0], halo_r.at[0], before_peer,
    )
    last_out = remote(
        basis.at[pl.ds(rows - layer, layer)], ext.at[pl.ds(0, layer)],
        halo_s.at[1], halo_r.at[1], after_peer,
    )
    lower_out = remote(
        stiff.at[cells - 1, pl.ds(layer, layer)], stiff_p,
        halo_s.at[2], halo_r.at[2], after_peer,
    )

    @pl.when(here > 0)
    def _():
        first_out.start()

    @pl.when(here < count - 1)
    def _():
        last_out.start()
        lower_out.start()

    for load in loads:
        load.wait()

    def halo_in():
        @pl.when(here > 0)
        def _():
            last_out.wait_recv()
            lower_out.wait_recv()

        @pl.when(here == 0)
        def _():
            ext[pl.ds(0, layer), :] = jnp.zeros((layer, width), BF16)
            stiff_p[...] = jnp.zeros(stiff_p.shape, BF16)

        @pl.when(here < count - 1)
        def _():
            first_out.wait_recv()

        @pl.when(here == count - 1)
        def _():
            ext[pl.ds(layer + rows, layer), :] = jnp.zeros((layer, width), BF16)

    def stiff_chunk(j):
        cols = pl.ds(j * chunk, chunk)
        carry = jnp.dot(stiff_p[...], ext[pl.ds(0, 2 * layer), cols], preferred_element_type=F32)
        for c in range(cells):
            at = c * layer
            prod = jnp.dot(
                stiff_v[c], ext[pl.ds(at + layer, 2 * layer), cols], preferred_element_type=F32
            )
            acted[pl.ds(at, layer), cols] = (prod[:layer] + carry).astype(BF16)
            carry = prod[layer:]

    def soft_chunk(j):
        cols = pl.ds(j * chunk, chunk)
        for c in range(cells):
            at = c * layer
            masked = soft_v[c] * mask_v[c].astype(F32).astype(BF16)
            prod = jnp.dot(
                masked, ext[pl.ds(at + layer, layer), cols], preferred_element_type=F32
            )
            softened[pl.ds(at, layer), cols] = prod.astype(BF16)

    def project(right, j):
        return lax.dot_general(
            ext[pl.ds(layer, rows), :], right[:, pl.ds(j * chunk, chunk)],
            (((0,), (0,)), ((), ())), preferred_element_type=F32,
        )

    kc = [remote(k_core_s.at[j, 1 - core], k_core_r.at[j], kc_s.at[j], kc_r.at[j], core_peer)
          for j in range(chunks)]
    kx = [remote(k_x_s.at[j], k_x_r.at[j], kx_s.at[j], kx_r.at[j], x_peer) for j in range(chunks)]
    kz = [[remote(k_z_s.at[j, d], k_z_r.at[j, d], kz_s.at[j, d], kz_r.at[j, d], z_peers[d])
           for d in range(nz - 1)] for j in range(chunks)]
    ec = [remote(e_core_s.at[j, 1 - core], e_core_r.at[j], ec_s.at[j], ec_r.at[j], core_peer)
          for j in range(chunks)]
    ex = [remote(e_x_s.at[j], e_x_r.at[j], ex_s.at[j], ex_r.at[j], x_peer) for j in range(chunks)]

    def k_start(j):
        part = project(acted, j)
        for c in range(2):
            for xx in range(2):
                for zz in range(nz):
                    at = ((zz * 2 + xx) * 2 + c) * k_rows
                    block = part[at:at + k_rows]
                    k_own[j, c, xx, zz] = block
                    k_core_s[j, c, xx, zz] = block.astype(BF16)
        kc[j].start()

    def k_across(j):
        kc[j].wait_recv()
        k_x_s[j] = (k_own[j, core, 1 - x] + k_core_r[j, 1 - x].astype(F32)).astype(BF16)
        kx[j].start()
        k_own[j, core, x] = k_own[j, core, x] + k_core_r[j, x].astype(F32)

    def k_along(j):
        kx[j].wait_recv()
        for d in range(nz - 1):
            to = (z + d + 1) % nz
            k_z_s[j, d] = (k_own[j, core, x, to] + k_x_r[j, to].astype(F32)).astype(BF16)
            kz[j][d].start()

    def k_end(j):
        total = k_own[j, core, x, z] + k_x_r[j, z].astype(F32)
        for d in range(nz - 1):
            kz[j][d].wait_recv()
            total = total + k_z_r[j, d].astype(F32)
        k_out[:, pl.ds(j * chunk, chunk)] = total

    def e_start(j):
        part = project(softened, j)
        for c in range(2):
            for xx in range(2):
                at = (xx * 2 + c) * e_rows
                block = part[at:at + e_rows]
                e_own[j, c, xx] = block
                e_core_s[j, c, xx] = block.astype(BF16)
        ec[j].start()

    def e_across(j):
        ec[j].wait_recv()
        e_x_s[j] = (e_own[j, core, 1 - x] + e_core_r[j, 1 - x].astype(F32)).astype(BF16)
        ex[j].start()

    def e_end(j):
        mine = e_own[j, core, x] + e_core_r[j, x].astype(F32)
        ex[j].wait_recv()
        e_out[:, pl.ds(j * chunk, chunk)] = mine + ex_in(j)

    def ex_in(j):
        return e_x_r[j].astype(F32)

    soft_chunk(0)
    e_start(0)
    halo_in()
    stiff_chunk(0)
    k_start(0)
    e_across(0)
    stiff_chunk(1)
    k_across(0)
    k_start(1)
    soft_chunk(1)
    k_across(1)
    e_start(1)
    k_along(0)
    e_end(0)
    e_across(1)
    k_along(1)
    k_end(0)
    k_end(1)
    e_end(1)

    @pl.when(here > 0)
    def _():
        first_out.wait_send()

    @pl.when(here < count - 1)
    def _():
        last_out.wait_send()
        lower_out.wait_send()

    for j in range(chunks):
        kc[j].wait_send()
        kx[j].wait_send()
        for d in range(nz - 1):
            kz[j][d].wait_send()
        ec[j].wait_send()
        ex[j].wait_send()


def fused_body(basis, stiff, soft, under):
    cells, layer, width = basis.shape
    rows = cells * layer
    nz = lax.axis_size("slab") // 2
    chunk = 256
    chunks = width // chunk
    k_rows = width // (4 * nz)
    e_rows = width // 4
    hbm = pl.BlockSpec(memory_space=pltpu.HBM)
    vmem = pl.BlockSpec(memory_space=pltpu.VMEM)
    dma = pltpu.SemaphoreType.DMA
    return pl.pallas_call(
        functools.partial(fused_kernel, nz, cells, layer, width, chunk),
        out_shape=(
            jax.ShapeDtypeStruct((k_rows, width), F32),
            jax.ShapeDtypeStruct((e_rows, width), F32),
        ),
        in_specs=[hbm] * 4,
        out_specs=(vmem, vmem),
        scratch_shapes=[
            pltpu.VMEM((rows + 2 * layer, width), BF16),
            pltpu.VMEM((cells, 2 * layer, 2 * layer), BF16),
            pltpu.VMEM((layer, 2 * layer), BF16),
            pltpu.VMEM((cells, layer, layer), BF16),
            pltpu.SMEM((cells,), jnp.int32),
            pltpu.VMEM((rows, width), BF16),
            pltpu.VMEM((rows, width), BF16),
            pltpu.VMEM((chunks, 2, 2, nz, k_rows, chunk), F32),
            pltpu.VMEM((chunks, 2, 2, nz, k_rows, chunk), BF16),
            pltpu.VMEM((chunks, 2, nz, k_rows, chunk), BF16),
            pltpu.VMEM((chunks, nz, k_rows, chunk), BF16),
            pltpu.VMEM((chunks, nz, k_rows, chunk), BF16),
            pltpu.VMEM((chunks, nz - 1, k_rows, chunk), BF16),
            pltpu.VMEM((chunks, nz - 1, k_rows, chunk), BF16),
            pltpu.VMEM((chunks, 2, 2, e_rows, chunk), F32),
            pltpu.VMEM((chunks, 2, 2, e_rows, chunk), BF16),
            pltpu.VMEM((chunks, 2, e_rows, chunk), BF16),
            pltpu.VMEM((chunks, e_rows, chunk), BF16),
            pltpu.VMEM((chunks, e_rows, chunk), BF16),
            dma((4,)), dma((3,)), dma((3,)),
            dma((chunks,)), dma((chunks,)), dma((chunks,)), dma((chunks,)),
            dma((chunks, nz - 1)), dma((chunks, nz - 1)),
            dma((chunks,)), dma((chunks,)), dma((chunks,)), dma((chunks,)),
        ],
        compiler_params=pltpu.CompilerParams(
            collective_id=0, has_side_effects=True, vmem_limit_bytes=60 << 20
        ),
        name="fused",
    )(basis.reshape(rows, width), stiff, soft, under)


def solution(mesh):
    placed = (
        P(("groups", "slab", "cross"), None, None),
        P(("groups", "slab", "cross"), None, None),
        P(("groups", "slab", "cross"), None, None),
        P(("groups", "slab", "cross")),
    )

    def body(basis, stiff, soft, under):
        cells, layer, width = basis.shape
        members = mesh.shape["slab"] * mesh.shape["cross"]
        fits = (
            mesh.shape["cross"] == 2
            and mesh.shape["slab"] % 2 == 0
            and mesh.shape["slab"] >= 4
            and width == 512
            and layer == 64
            and cells % 4 == 0
            and (cells * layer) % 256 == 0
            and width // members >= 16
            and (width // members) % 16 == 0
        )
        return (fused_body if fits else plain_body)(basis, stiff, soft, under)

    return jax.shard_map(
        body,
        mesh=mesh,
        in_specs=placed,
        out_specs=(P(("groups", "slab", "cross"), None), P(("groups", "slab", "cross"), None)),
        check_vma=False,
    )
```

```python
import functools

import jax
import jax.numpy as jnp
from jax import lax
from jax.experimental import pallas as pl
from jax.experimental.pallas import tpu as pltpu
from jax.sharding import PartitionSpec as P

MESH = pl.DeviceIdType.MESH
BF16 = jnp.bfloat16
F32 = jnp.float32


def shifted(x, axis, by):
    length = lax.axis_size(axis)
    pairs = [(i, i + by) for i in range(length) if 0 <= i + by < length]
    return lax.ppermute(x, axis, pairs)


def partner(x, axis, bit):
    return lax.ppermute(x, axis, [(i, i ^ 1 << bit) for i in range(lax.axis_size(axis))])


def plain_body(basis, stiff, soft, under):
    cells, layer, width = basis.shape
    nextcell = shifted(basis[:1], ("slab", "cross"), -1)
    upper_cells = jnp.concatenate([basis[1:], nextcell], axis=0)
    pairs = jnp.concatenate([basis, upper_cells], axis=1)
    prod = jnp.einsum("cij,cjr->cir", stiff, pairs, preferred_element_type=jnp.float32)
    carry_in = shifted(prod[-1:, layer:], ("slab", "cross"), 1)
    action = prod[:, :layer] + jnp.concatenate([carry_in, prod[:-1, layer:]], axis=0)
    flat_basis = basis.reshape(cells * layer, width)
    flat_stiff = action.astype(jnp.bfloat16).reshape(cells * layer, width)
    k_reduced = lax.psum_scatter(
        lax.dot_general(
            flat_basis, flat_stiff, (((0,), (0,)), ((), ())), preferred_element_type=jnp.float32
        ),
        ("slab", "cross"),
        scatter_dimension=0,
        tiled=True,
    )
    masked = soft * under.astype(jnp.bfloat16)[:, None, None]
    soft_basis = jnp.einsum("cij,cjr->cir", masked, basis, preferred_element_type=jnp.float32)
    flat_soft = soft_basis.astype(jnp.bfloat16).reshape(cells * layer, width)
    partial_sum = lax.dot_general(
        flat_basis, flat_soft, (((0,), (0,)), ((), ())), preferred_element_type=jnp.float32
    )
    parity = lax.axis_index("slab") % 2
    halves = partial_sum.reshape(2, width // 2, width)
    mine = lax.dynamic_index_in_dim(halves, parity, 0, keepdims=False)
    other = lax.dynamic_index_in_dim(halves, 1 - parity, 0, keepdims=False)
    paired = mine + partner(other, "slab", 0)
    electrode_rows = lax.psum_scatter(paired, "cross", scatter_dimension=0, tiled=True)
    return (k_reduced, electrode_rows)


def fused_kernel(
    nz, cells, layer, width, chunk,
    basis, stiff, soft, under, k_out, e_out,
    ext, stiff_v, stiff_p, soft_v, mask_v, acted, softened, held,
    k_own, k_core_s, k_core_r, k_s, k_r, k_res,
    e_own, e_core_s, e_core_r, e_x_s, e_x_r, e_res,
    load_sem, halo_s, halo_r, kc_s, kc_r, kp_s, kp_r, ec_s, ec_r, ex_s, ex_r, ko_sem, eo_sem,
):
    slab = lax.axis_index("slab")
    core = lax.axis_index("cross")
    z, x = slab // 2, slab % 2
    here = slab * 2 + core
    count = nz * 4
    rows = cells * layer
    chunks = width // chunk
    k_rows = width // count
    e_rows = width // 4

    core_peer = {"cross": 1 - core}
    x_peer = {"slab": slab + 1 - 2 * x}
    turns = [nz // 2] + [d for d in range(1, nz) if d != nz // 2]
    places = [((z + d) % nz, (x + e) % 2) for d in turns for e in (1, 0)] + [(z, 1 - x)]
    chip_peers = [{"slab": zz * 2 + xx} for zz, xx in places]
    before = (here + count - 1) % count
    after = (here + 1) % count
    before_peer = {"slab": before // 2, "cross": before % 2}
    after_peer = {"slab": after // 2, "cross": after % 2}

    barrier = pltpu.get_barrier_semaphore()
    peers = [*chip_peers, core_peer, before_peer, after_peer]
    for peer in peers:
        pl.semaphore_signal(barrier, inc=1, device_id=peer, device_id_type=MESH)

    loads = [
        pltpu.make_async_copy(under, mask_v, load_sem.at[3]),
        pltpu.make_async_copy(soft, soft_v, load_sem.at[2]),
        pltpu.make_async_copy(basis, ext.at[pl.ds(layer, rows)], load_sem.at[0]),
        pltpu.make_async_copy(stiff, stiff_v, load_sem.at[1]),
    ]
    for load in loads:
        load.start()

    def remote(src, dst, send, recv, peer):
        return pltpu.make_async_remote_copy(
            src_ref=src, dst_ref=dst, send_sem=send, recv_sem=recv,
            device_id=peer, device_id_type=MESH,
        )

    first_out = remote(
        basis.at[pl.ds(0, layer)], ext.at[pl.ds(layer + rows, layer)],
        halo_s.at[0], halo_r.at[0], before_peer,
    )
    last_out = remote(
        basis.at[pl.ds(rows - layer, layer)], ext.at[pl.ds(0, layer)],
        halo_s.at[1], halo_r.at[1], after_peer,
    )
    lower_out = remote(
        stiff.at[cells - 1, pl.ds(layer, layer)], stiff_p,
        halo_s.at[2], halo_r.at[2], after_peer,
    )

    def halo_out():
        @pl.when(here > 0)
        def _():
            first_out.start()

        @pl.when(here < count - 1)
        def _():
            last_out.start()
            lower_out.start()

    def halo_in():
        @pl.when(here > 0)
        def _():
            last_out.wait_recv()
            lower_out.wait_recv()

        @pl.when(here == 0)
        def _():
            ext[pl.ds(0, layer), :] = jnp.zeros((layer, width), BF16)
            stiff_p[...] = jnp.zeros(stiff_p.shape, BF16)

        @pl.when(here < count - 1)
        def _():
            first_out.wait_recv()

        @pl.when(here == count - 1)
        def _():
            ext[pl.ds(layer + rows, layer), :] = jnp.zeros((layer, width), BF16)

    def across(left, right):
        return lax.dot_general(
            left, right, (((0,), (0,)), ((), ())), preferred_element_type=F32
        )

    def stiff_inner(j):
        cols = pl.ds(j * chunk, chunk)
        carry = None
        for c in range(cells - 1):
            at = c * layer
            prod = jnp.dot(
                stiff_v[c], ext[pl.ds(at + layer, 2 * layer), cols], preferred_element_type=F32
            )
            if c == 0:
                held[0, :, cols] = prod[:layer]
            else:
                acted[pl.ds(at, layer), cols] = (prod[:layer] + carry).astype(BF16)
            carry = prod[layer:]
        held[1, :, cols] = carry

    def soft_chunk(j):
        cols = pl.ds(j * chunk, chunk)
        for c in range(cells):
            at = c * layer
            masked = soft_v[c] * mask_v[c].astype(F32).astype(BF16)
            prod = jnp.dot(
                masked, ext[pl.ds(at + layer, layer), cols], preferred_element_type=F32
            )
            softened[pl.ds(at, layer), cols] = prod.astype(BF16)

    kc = [remote(k_core_s.at[j, 1 - core], k_core_r.at[j], kc_s.at[j], kc_r.at[j], core_peer)
          for j in range(chunks)]
    kp = [[remote(k_s.at[j, p], k_r.at[j, p], kp_s.at[j, p], kp_r.at[j, p], peer)
           for p, peer in enumerate(chip_peers)] for j in range(chunks)]
    ec = [remote(e_core_s.at[j, 1 - core], e_core_r.at[j], ec_s.at[j], ec_r.at[j], core_peer)
          for j in range(chunks)]
    ex = [remote(e_x_s.at[j], e_x_r.at[j], ex_s.at[j], ex_r.at[j], x_peer) for j in range(chunks)]
    ko = [pltpu.make_async_copy(k_res.at[j], k_out.at[:, pl.ds(j * chunk, chunk)], ko_sem.at[j])
          for j in range(chunks)]
    eo = [pltpu.make_async_copy(e_res.at[j], e_out.at[:, pl.ds(j * chunk, chunk)], eo_sem.at[j])
          for j in range(chunks)]

    def k_blocks():
        for c in range(2):
            for xx in range(2):
                for zz in range(nz):
                    yield c, xx, zz, ((zz * 2 + xx) * 2 + c) * k_rows

    def k_inner(j):
        part = across(
            ext[pl.ds(2 * layer, rows - 2 * layer), :],
            acted[pl.ds(layer, rows - 2 * layer), pl.ds(j * chunk, chunk)],
        )
        for c, xx, zz, at in k_blocks():
            k_own[j, c, xx, zz] = part[at:at + k_rows]

    def k_start(j):
        cols = pl.ds(j * chunk, chunk)
        low = held[0, :, cols] + jnp.dot(
            stiff_p[...], ext[pl.ds(0, 2 * layer), cols], preferred_element_type=F32
        )
        high = held[1, :, cols] + jnp.dot(
            stiff_v[cells - 1, pl.ds(0, layer)], ext[pl.ds(rows, 2 * layer), cols],
            preferred_element_type=F32,
        )
        part = across(
            jnp.concatenate([ext[pl.ds(layer, layer), :], ext[pl.ds(rows, layer), :]], axis=0),
            jnp.concatenate([low.astype(BF16), high.astype(BF16)], axis=0),
        )
        for c, xx, zz, at in k_blocks():
            block = k_own[j, c, xx, zz] + part[at:at + k_rows]
            k_own[j, c, xx, zz] = block
            k_core_s[j, c, xx, zz] = block.astype(BF16)
        kc[j].start()

    def k_across(j):
        kc[j].wait_recv()
        for p, (zz, xx) in enumerate(places):
            k_s[j, p] = (k_own[j, core, xx, zz] + k_core_r[j, xx, zz].astype(F32)).astype(BF16)
            kp[j][p].start()

    def k_end(j):
        total = k_own[j, core, x, z] + k_core_r[j, x, z].astype(F32)
        for p in reversed(range(len(places))):
            kp[j][p].wait_recv()
            total = total + k_r[j, p].astype(F32)
        k_res[j] = total
        ko[j].start()

    def e_inner(j):
        part = across(ext[pl.ds(layer, rows), :], softened[:, pl.ds(j * chunk, chunk)])
        for c in range(2):
            for xx in range(2):
                at = (xx * 2 + c) * e_rows
                block = part[at:at + e_rows]
                e_own[j, c, xx] = block
                e_core_s[j, c, xx] = block.astype(BF16)

    def e_across(j):
        ec[j].wait_recv()
        e_x_s[j] = (e_own[j, core, 1 - x] + e_core_r[j, 1 - x].astype(F32)).astype(BF16)
        ex[j].start()

    def e_end(j):
        mine = e_own[j, core, x] + e_core_r[j, x].astype(F32)
        ex[j].wait_recv()
        e_res[j] = mine + e_x_r[j].astype(F32)
        eo[j].start()

    for load in loads[:3]:
        load.wait()
    soft_chunk(0)
    e_inner(0)
    pl.semaphore_wait(barrier, len(peers))
    halo_out()
    ec[0].start()
    loads[3].wait()
    stiff_inner(0)
    k_inner(0)
    e_across(0)
    stiff_inner(1)
    k_inner(1)
    soft_chunk(1)
    halo_in()
    k_start(0)
    k_start(1)
    e_inner(1)
    ec[1].start()
    k_across(0)
    k_across(1)
    e_across(1)
    e_end(0)
    e_end(1)
    k_end(0)
    k_end(1)

    @pl.when(here > 0)
    def _():
        first_out.wait_send()

    @pl.when(here < count - 1)
    def _():
        last_out.wait_send()
        lower_out.wait_send()

    for j in range(chunks):
        kc[j].wait_send()
        for copy in kp[j]:
            copy.wait_send()
        ec[j].wait_send()
        ex[j].wait_send()
        eo[j].wait()
        ko[j].wait()


def hand_on(k_in, e_in, k_out, e_out, k_v, e_v, sem):
    parts = 2
    size = e_v.shape[0] // parts
    reads = [pltpu.make_async_copy(e_in.at[pl.ds(i * size, size)], e_v.at[pl.ds(i * size, size)],
                                   sem.at[0, i]) for i in range(parts)]
    writes = [pltpu.make_async_copy(e_v.at[pl.ds(i * size, size)], e_out.at[pl.ds(i * size, size)],
                                    sem.at[1, i]) for i in range(parts)]
    reads.append(pltpu.make_async_copy(k_in, k_v, sem.at[0, parts]))
    writes.append(pltpu.make_async_copy(k_v, k_out, sem.at[1, parts]))
    for copy in reads:
        copy.start()
    for read, write in zip(reads, writes):
        read.wait()
        write.start()
    for copy in writes:
        copy.wait()


def fused_body(basis, stiff, soft, under):
    cells, layer, width = basis.shape
    rows = cells * layer
    nz = lax.axis_size("slab") // 2
    chunk = 256
    chunks = width // chunk
    k_rows = width // (4 * nz)
    e_rows = width // 4
    others = 2 * nz - 1
    hbm = pl.BlockSpec(memory_space=pl.ANY)
    dma = pltpu.SemaphoreType.DMA
    shapes = (
        jax.ShapeDtypeStruct((k_rows, width), F32),
        jax.ShapeDtypeStruct((e_rows, width), F32),
    )
    k_red, e_red = pl.pallas_call(
        functools.partial(fused_kernel, nz, cells, layer, width, chunk),
        out_shape=shapes,
        in_specs=[hbm] * 4,
        out_specs=(hbm, hbm),
        scratch_shapes=[
            pltpu.VMEM((rows + 2 * layer, width), BF16),
            pltpu.VMEM((cells, 2 * layer, 2 * layer), BF16),
            pltpu.VMEM((layer, 2 * layer), BF16),
            pltpu.VMEM((cells, layer, layer), BF16),
            pltpu.SMEM((cells,), jnp.int32),
            pltpu.VMEM((rows, width), BF16),
            pltpu.VMEM((rows, width), BF16),
            pltpu.VMEM((2, layer, width), F32),
            pltpu.VMEM((chunks, 2, 2, nz, k_rows, chunk), F32),
            pltpu.VMEM((chunks, 2, 2, nz, k_rows, chunk), BF16),
            pltpu.VMEM((chunks, 2, nz, k_rows, chunk), BF16),
            pltpu.VMEM((chunks, others, k_rows, chunk), BF16),
            pltpu.VMEM((chunks, others, k_rows, chunk), BF16),
            pltpu.VMEM((chunks, k_rows, chunk), F32),
            pltpu.VMEM((chunks, 2, 2, e_rows, chunk), F32),
            pltpu.VMEM((chunks, 2, 2, e_rows, chunk), BF16),
            pltpu.VMEM((chunks, 2, e_rows, chunk), BF16),
            pltpu.VMEM((chunks, e_rows, chunk), BF16),
            pltpu.VMEM((chunks, e_rows, chunk), BF16),
            pltpu.VMEM((chunks, e_rows, chunk), F32),
            dma((4,)), dma((3,)), dma((3,)),
            dma((chunks,)), dma((chunks,)),
            dma((chunks, others)), dma((chunks, others)),
            dma((chunks,)), dma((chunks,)), dma((chunks,)), dma((chunks,)),
            dma((chunks,)), dma((chunks,)),
        ],
        compiler_params=pltpu.CompilerParams(
            collective_id=0, has_side_effects=True, vmem_limit_bytes=60 << 20
        ),
        name="fused",
    )(basis.reshape(rows, width), stiff, soft, under)
    return pl.pallas_call(
        hand_on,
        out_shape=shapes,
        in_specs=[hbm, hbm],
        out_specs=(hbm, hbm),
        scratch_shapes=[
            pltpu.VMEM(shapes[0].shape, F32), pltpu.VMEM(shapes[1].shape, F32), dma((2, 3)),
        ],
        compiler_params=pltpu.CompilerParams(vmem_limit_bytes=60 << 20),
        name="hand_on",
    )(k_red, e_red)


def solution(mesh):
    placed = (
        P(("groups", "slab", "cross"), None, None),
        P(("groups", "slab", "cross"), None, None),
        P(("groups", "slab", "cross"), None, None),
        P(("groups", "slab", "cross")),
    )

    def body(basis, stiff, soft, under):
        cells, layer, width = basis.shape
        members = mesh.shape["slab"] * mesh.shape["cross"]
        fits = (
            mesh.shape["cross"] == 2
            and mesh.shape["slab"] % 2 == 0
            and mesh.shape["slab"] >= 4
            and width == 512
            and layer == 64
            and cells % 4 == 0
            and (cells * layer) % 256 == 0
            and width // members >= 16
            and (width // members) % 16 == 0
        )
        return (fused_body if fits else plain_body)(basis, stiff, soft, under)

    return jax.shard_map(
        body,
        mesh=mesh,
        in_specs=placed,
        out_specs=(P(("groups", "slab", "cross"), None), P(("groups", "slab", "cross"), None)),
        check_vma=False,
    )
```

```python
import functools

import jax
import jax.numpy as jnp
from jax import lax
from jax.experimental import pallas as pl
from jax.experimental.pallas import tpu as pltpu
from jax.sharding import PartitionSpec as P

MESH = pl.DeviceIdType.MESH
BF16 = jnp.bfloat16
F32 = jnp.float32


def shifted(x, axis, by):
    length = lax.axis_size(axis)
    pairs = [(i, i + by) for i in range(length) if 0 <= i + by < length]
    return lax.ppermute(x, axis, pairs)


def partner(x, axis, bit):
    return lax.ppermute(x, axis, [(i, i ^ 1 << bit) for i in range(lax.axis_size(axis))])


def plain_body(basis, stiff, soft, under):
    cells, layer, width = basis.shape
    nextcell = shifted(basis[:1], ("slab", "cross"), -1)
    upper_cells = jnp.concatenate([basis[1:], nextcell], axis=0)
    pairs = jnp.concatenate([basis, upper_cells], axis=1)
    prod = jnp.einsum("cij,cjr->cir", stiff, pairs, preferred_element_type=jnp.float32)
    carry_in = shifted(prod[-1:, layer:], ("slab", "cross"), 1)
    action = prod[:, :layer] + jnp.concatenate([carry_in, prod[:-1, layer:]], axis=0)
    flat_basis = basis.reshape(cells * layer, width)
    flat_stiff = action.astype(jnp.bfloat16).reshape(cells * layer, width)
    k_reduced = lax.psum_scatter(
        lax.dot_general(
            flat_basis, flat_stiff, (((0,), (0,)), ((), ())), preferred_element_type=jnp.float32
        ),
        ("slab", "cross"),
        scatter_dimension=0,
        tiled=True,
    )
    masked = soft * under.astype(jnp.bfloat16)[:, None, None]
    soft_basis = jnp.einsum("cij,cjr->cir", masked, basis, preferred_element_type=jnp.float32)
    flat_soft = soft_basis.astype(jnp.bfloat16).reshape(cells * layer, width)
    partial_sum = lax.dot_general(
        flat_basis, flat_soft, (((0,), (0,)), ((), ())), preferred_element_type=jnp.float32
    )
    parity = lax.axis_index("slab") % 2
    halves = partial_sum.reshape(2, width // 2, width)
    mine = lax.dynamic_index_in_dim(halves, parity, 0, keepdims=False)
    other = lax.dynamic_index_in_dim(halves, 1 - parity, 0, keepdims=False)
    paired = mine + partner(other, "slab", 0)
    electrode_rows = lax.psum_scatter(paired, "cross", scatter_dimension=0, tiled=True)
    return (k_reduced, electrode_rows)


def fused_kernel(
    nz, cells, layer, width, chunk,
    basis, stiff, soft, under, k_out, e_out,
    ext, stiff_v, stiff_p, soft_v, mask_v, acted, softened, held,
    k_own, k_core_s, k_core_r, k_s, k_r,
    e_own, e_core_s, e_core_r, e_x_s, e_x_r,
    load_sem, halo_s, halo_r, kc_s, kc_r, kp_s, kp_r, ec_s, ec_r, ex_s, ex_r,
):
    slab = lax.axis_index("slab")
    core = lax.axis_index("cross")
    z, x = slab // 2, slab % 2
    here = slab * 2 + core
    count = nz * 4
    rows = cells * layer
    chunks = width // chunk
    k_rows = width // count
    e_rows = width // 4

    core_peer = {"cross": 1 - core}
    x_peer = {"slab": slab + 1 - 2 * x}
    turns = [nz // 2] + [d for d in range(1, nz) if d != nz // 2]
    places = [((z + d) % nz, (x + e) % 2) for d in turns for e in (1, 0)] + [(z, 1 - x)]
    chip_peers = [{"slab": zz * 2 + xx} for zz, xx in places]
    before = (here + count - 1) % count
    after = (here + 1) % count
    before_peer = {"slab": before // 2, "cross": before % 2}
    after_peer = {"slab": after // 2, "cross": after % 2}

    barrier = pltpu.get_barrier_semaphore()
    peers = [*chip_peers, core_peer, before_peer, after_peer]
    for peer in peers:
        pl.semaphore_signal(barrier, inc=1, device_id=peer, device_id_type=MESH)

    loads = [
        pltpu.make_async_copy(under, mask_v, load_sem.at[3]),
        pltpu.make_async_copy(soft, soft_v, load_sem.at[2]),
        pltpu.make_async_copy(basis, ext.at[pl.ds(layer, rows)], load_sem.at[0]),
        pltpu.make_async_copy(stiff, stiff_v, load_sem.at[1]),
    ]
    for load in loads:
        load.start()

    def remote(src, dst, send, recv, peer):
        return pltpu.make_async_remote_copy(
            src_ref=src, dst_ref=dst, send_sem=send, recv_sem=recv,
            device_id=peer, device_id_type=MESH,
        )

    first_out = remote(
        basis.at[pl.ds(0, layer)], ext.at[pl.ds(layer + rows, layer)],
        halo_s.at[0], halo_r.at[0], before_peer,
    )
    last_out = remote(
        basis.at[pl.ds(rows - layer, layer)], ext.at[pl.ds(0, layer)],
        halo_s.at[1], halo_r.at[1], after_peer,
    )
    lower_out = remote(
        stiff.at[cells - 1, pl.ds(layer, layer)], stiff_p,
        halo_s.at[2], halo_r.at[2], after_peer,
    )

    def halo_out():
        @pl.when(here > 0)
        def _():
            first_out.start()

        @pl.when(here < count - 1)
        def _():
            last_out.start()
            lower_out.start()

    def halo_in():
        @pl.when(here > 0)
        def _():
            last_out.wait_recv()
            lower_out.wait_recv()

        @pl.when(here == 0)
        def _():
            ext[pl.ds(0, layer), :] = jnp.zeros((layer, width), BF16)
            stiff_p[...] = jnp.zeros(stiff_p.shape, BF16)

        @pl.when(here < count - 1)
        def _():
            first_out.wait_recv()

        @pl.when(here == count - 1)
        def _():
            ext[pl.ds(layer + rows, layer), :] = jnp.zeros((layer, width), BF16)

    def across(left, right):
        return lax.dot_general(
            left, right, (((0,), (0,)), ((), ())), preferred_element_type=F32
        )

    def stiff_inner(j):
        cols = pl.ds(j * chunk, chunk)
        carry = None
        for c in range(cells - 1):
            at = c * layer
            prod = jnp.dot(
                stiff_v[c], ext[pl.ds(at + layer, 2 * layer), cols], preferred_element_type=F32
            )
            if c == 0:
                held[0, :, cols] = prod[:layer]
            else:
                acted[pl.ds(at, layer), cols] = (prod[:layer] + carry).astype(BF16)
            carry = prod[layer:]
        held[1, :, cols] = carry

    def soft_chunk(j):
        cols = pl.ds(j * chunk, chunk)
        for c in range(cells):
            at = c * layer
            masked = soft_v[c] * mask_v[c].astype(F32).astype(BF16)
            prod = jnp.dot(
                masked, ext[pl.ds(at + layer, layer), cols], preferred_element_type=F32
            )
            softened[pl.ds(at, layer), cols] = prod.astype(BF16)

    kc = [remote(k_core_s.at[j, 1 - core], k_core_r.at[j], kc_s.at[j], kc_r.at[j], core_peer)
          for j in range(chunks)]
    kp = [[remote(k_s.at[j, p], k_r.at[j, p], kp_s.at[j, p], kp_r.at[j, p], peer)
           for p, peer in enumerate(chip_peers)] for j in range(chunks)]
    ec = [remote(e_core_s.at[j, 1 - core], e_core_r.at[j], ec_s.at[j], ec_r.at[j], core_peer)
          for j in range(chunks)]
    ex = [remote(e_x_s.at[j], e_x_r.at[j], ex_s.at[j], ex_r.at[j], x_peer) for j in range(chunks)]

    def k_blocks():
        for c in range(2):
            for xx in range(2):
                for zz in range(nz):
                    yield c, xx, zz, ((zz * 2 + xx) * 2 + c) * k_rows

    def k_inner(j):
        part = across(
            ext[pl.ds(2 * layer, rows - 2 * layer), :],
            acted[pl.ds(layer, rows - 2 * layer), pl.ds(j * chunk, chunk)],
        )
        for c, xx, zz, at in k_blocks():
            k_own[j, c, xx, zz] = part[at:at + k_rows]

    def k_start(j):
        cols = pl.ds(j * chunk, chunk)
        low = held[0, :, cols] + jnp.dot(
            stiff_p[...], ext[pl.ds(0, 2 * layer), cols], preferred_element_type=F32
        )
        high = held[1, :, cols] + jnp.dot(
            stiff_v[cells - 1, pl.ds(0, layer)], ext[pl.ds(rows, 2 * layer), cols],
            preferred_element_type=F32,
        )
        part = across(
            jnp.concatenate([ext[pl.ds(layer, layer), :], ext[pl.ds(rows, layer), :]], axis=0),
            jnp.concatenate([low.astype(BF16), high.astype(BF16)], axis=0),
        )
        for c, xx, zz, at in k_blocks():
            block = k_own[j, c, xx, zz] + part[at:at + k_rows]
            k_own[j, c, xx, zz] = block
            k_core_s[j, c, xx, zz] = block.astype(BF16)
        kc[j].start()

    def k_across(j):
        kc[j].wait_recv()
        for p, (zz, xx) in enumerate(places):
            k_s[j, p] = (k_own[j, core, xx, zz] + k_core_r[j, xx, zz].astype(F32)).astype(BF16)
            kp[j][p].start()

    def k_end(j):
        total = k_own[j, core, x, z] + k_core_r[j, x, z].astype(F32)
        for p in reversed(range(len(places))):
            kp[j][p].wait_recv()
            total = total + k_r[j, p].astype(F32)
        k_out[:, pl.ds(j * chunk, chunk)] = total

    def e_inner(j):
        part = across(ext[pl.ds(layer, rows), :], softened[:, pl.ds(j * chunk, chunk)])
        for c in range(2):
            for xx in range(2):
                at = (xx * 2 + c) * e_rows
                block = part[at:at + e_rows]
                e_own[j, c, xx] = block
                e_core_s[j, c, xx] = block.astype(BF16)

    def e_across(j):
        ec[j].wait_recv()
        e_x_s[j] = (e_own[j, core, 1 - x] + e_core_r[j, 1 - x].astype(F32)).astype(BF16)
        ex[j].start()

    def e_end(j):
        mine = e_own[j, core, x] + e_core_r[j, x].astype(F32)
        ex[j].wait_recv()
        e_out[:, pl.ds(j * chunk, chunk)] = mine + e_x_r[j].astype(F32)

    for load in loads[:3]:
        load.wait()
    soft_chunk(0)
    e_inner(0)
    pl.semaphore_wait(barrier, len(peers))
    halo_out()
    ec[0].start()
    loads[3].wait()
    stiff_inner(0)
    k_inner(0)
    e_across(0)
    stiff_inner(1)
    k_inner(1)
    soft_chunk(1)
    halo_in()
    k_start(0)
    k_start(1)
    e_inner(1)
    ec[1].start()
    k_across(0)
    k_across(1)
    e_across(1)
    e_end(0)
    e_end(1)
    k_end(0)
    k_end(1)

    @pl.when(here > 0)
    def _():
        first_out.wait_send()

    @pl.when(here < count - 1)
    def _():
        last_out.wait_send()
        lower_out.wait_send()

    for j in range(chunks):
        kc[j].wait_send()
        for copy in kp[j]:
            copy.wait_send()
        ec[j].wait_send()
        ex[j].wait_send()


def hand_on(k_in, e_in, k_out, e_out, sem):
    copies = [
        pltpu.make_async_copy(e_in, e_out, sem.at[0]),
        pltpu.make_async_copy(k_in, k_out, sem.at[1]),
    ]
    for copy in copies:
        copy.start()
    for copy in copies:
        copy.wait()


def fused_body(basis, stiff, soft, under):
    cells, layer, width = basis.shape
    rows = cells * layer
    nz = lax.axis_size("slab") // 2
    chunk = 256
    chunks = width // chunk
    k_rows = width // (4 * nz)
    e_rows = width // 4
    others = 2 * nz - 1
    hbm = pl.BlockSpec(memory_space=pl.ANY)
    vmem = pl.BlockSpec(memory_space=pltpu.VMEM)
    dma = pltpu.SemaphoreType.DMA
    shapes = (
        jax.ShapeDtypeStruct((k_rows, width), F32),
        jax.ShapeDtypeStruct((e_rows, width), F32),
    )
    k_red, e_red = pl.pallas_call(
        functools.partial(fused_kernel, nz, cells, layer, width, chunk),
        out_shape=(pltpu.VMEM((k_rows, width), F32), pltpu.VMEM((e_rows, width), F32)),
        in_specs=[hbm] * 4,
        out_specs=(vmem, vmem),
        scratch_shapes=[
            pltpu.VMEM((rows + 2 * layer, width), BF16),
            pltpu.VMEM((cells, 2 * layer, 2 * layer), BF16),
            pltpu.VMEM((layer, 2 * layer), BF16),
            pltpu.VMEM((cells, layer, layer), BF16),
            pltpu.SMEM((cells,), jnp.int32),
            pltpu.VMEM((rows, width), BF16),
            pltpu.VMEM((rows, width), BF16),
            pltpu.VMEM((2, layer, width), F32),
            pltpu.VMEM((chunks, 2, 2, nz, k_rows, chunk), F32),
            pltpu.VMEM((chunks, 2, 2, nz, k_rows, chunk), BF16),
            pltpu.VMEM((chunks, 2, nz, k_rows, chunk), BF16),
            pltpu.VMEM((chunks, others, k_rows, chunk), BF16),
            pltpu.VMEM((chunks, others, k_rows, chunk), BF16),
            pltpu.VMEM((chunks, 2, 2, e_rows, chunk), F32),
            pltpu.VMEM((chunks, 2, 2, e_rows, chunk), BF16),
            pltpu.VMEM((chunks, 2, e_rows, chunk), BF16),
            pltpu.VMEM((chunks, e_rows, chunk), BF16),
            pltpu.VMEM((chunks, e_rows, chunk), BF16),
            dma((4,)), dma((3,)), dma((3,)),
            dma((chunks,)), dma((chunks,)),
            dma((chunks, others)), dma((chunks, others)),
            dma((chunks,)), dma((chunks,)), dma((chunks,)), dma((chunks,)),
        ],
        compiler_params=pltpu.CompilerParams(
            collective_id=0, has_side_effects=True, vmem_limit_bytes=60 << 20
        ),
        name="fused",
    )(basis.reshape(rows, width), stiff, soft, under)
    return pl.pallas_call(
        hand_on,
        out_shape=shapes,
        in_specs=[vmem, vmem],
        out_specs=(hbm, hbm),
        scratch_shapes=[dma((2,))],
        compiler_params=pltpu.CompilerParams(vmem_limit_bytes=32 << 20),
        name="hand_on",
    )(k_red, e_red)


def solution(mesh):
    placed = (
        P(("groups", "slab", "cross"), None, None),
        P(("groups", "slab", "cross"), None, None),
        P(("groups", "slab", "cross"), None, None),
        P(("groups", "slab", "cross")),
    )

    def body(basis, stiff, soft, under):
        cells, layer, width = basis.shape
        members = mesh.shape["slab"] * mesh.shape["cross"]
        fits = (
            mesh.shape["cross"] == 2
            and mesh.shape["slab"] % 2 == 0
            and mesh.shape["slab"] >= 4
            and width == 512
            and layer == 64
            and cells % 4 == 0
            and (cells * layer) % 256 == 0
            and width // members >= 16
            and (width // members) % 16 == 0
        )
        return (fused_body if fits else plain_body)(basis, stiff, soft, under)

    return jax.shard_map(
        body,
        mesh=mesh,
        in_specs=placed,
        out_specs=(P(("groups", "slab", "cross"), None), P(("groups", "slab", "cross"), None)),
        check_vma=False,
    )
```

```python
import functools

import jax
import jax.numpy as jnp
from jax import lax
from jax.experimental import pallas as pl
from jax.experimental.pallas import tpu as pltpu
from jax.sharding import PartitionSpec as P

MESH = pl.DeviceIdType.MESH
BF16 = jnp.bfloat16
F32 = jnp.float32


def shifted(x, axis, by):
    length = lax.axis_size(axis)
    pairs = [(i, i + by) for i in range(length) if 0 <= i + by < length]
    return lax.ppermute(x, axis, pairs)


def partner(x, axis, bit):
    return lax.ppermute(x, axis, [(i, i ^ 1 << bit) for i in range(lax.axis_size(axis))])


def plain_body(basis, stiff, soft, under):
    cells, layer, width = basis.shape
    nextcell = shifted(basis[:1], ("slab", "cross"), -1)
    upper_cells = jnp.concatenate([basis[1:], nextcell], axis=0)
    pairs = jnp.concatenate([basis, upper_cells], axis=1)
    prod = jnp.einsum("cij,cjr->cir", stiff, pairs, preferred_element_type=jnp.float32)
    carry_in = shifted(prod[-1:, layer:], ("slab", "cross"), 1)
    action = prod[:, :layer] + jnp.concatenate([carry_in, prod[:-1, layer:]], axis=0)
    flat_basis = basis.reshape(cells * layer, width)
    flat_stiff = action.astype(jnp.bfloat16).reshape(cells * layer, width)
    k_reduced = lax.psum_scatter(
        lax.dot_general(
            flat_basis, flat_stiff, (((0,), (0,)), ((), ())), preferred_element_type=jnp.float32
        ),
        ("slab", "cross"),
        scatter_dimension=0,
        tiled=True,
    )
    masked = soft * under.astype(jnp.bfloat16)[:, None, None]
    soft_basis = jnp.einsum("cij,cjr->cir", masked, basis, preferred_element_type=jnp.float32)
    flat_soft = soft_basis.astype(jnp.bfloat16).reshape(cells * layer, width)
    partial_sum = lax.dot_general(
        flat_basis, flat_soft, (((0,), (0,)), ((), ())), preferred_element_type=jnp.float32
    )
    parity = lax.axis_index("slab") % 2
    halves = partial_sum.reshape(2, width // 2, width)
    mine = lax.dynamic_index_in_dim(halves, parity, 0, keepdims=False)
    other = lax.dynamic_index_in_dim(halves, 1 - parity, 0, keepdims=False)
    paired = mine + partner(other, "slab", 0)
    electrode_rows = lax.psum_scatter(paired, "cross", scatter_dimension=0, tiled=True)
    return (k_reduced, electrode_rows)


def fused_kernel(
    nz, cells, layer, width, chunk,
    basis, stiff, soft, under, k_out, e_out,
    ext, stiff_v, stiff_p, soft_v, mask_v, acted, softened, held,
    k_own, k_core_s, k_core_r, k_s, k_r,
    e_own, e_core_s, e_core_r, e_x_s, e_x_r,
    load_sem, halo_s, halo_r, kc_s, kc_r, kp_s, kp_r, ec_s, ec_r, ex_s, ex_r, told,
):
    slab = lax.axis_index("slab")
    core = lax.axis_index("cross")
    z, x = slab // 2, slab % 2
    here = slab * 2 + core
    count = nz * 4
    rows = cells * layer
    chunks = width // chunk
    k_rows = width // count
    e_rows = width // 4

    core_peer = {"cross": 1 - core}
    x_peer = {"slab": slab + 1 - 2 * x}
    turns = [nz // 2] + [d for d in range(1, nz) if d != nz // 2]
    places = [((z + d) % nz, (x + e) % 2) for d in turns for e in (1, 0)] + [(z, 1 - x)]
    chip_peers = [{"slab": zz * 2 + xx} for zz, xx in places]
    before = (here + count - 1) % count
    after = (here + 1) % count
    before_peer = {"slab": before // 2, "cross": before % 2}
    after_peer = {"slab": after // 2, "cross": after % 2}

    barrier = pltpu.get_barrier_semaphore()
    for peer in (core_peer, x_peer):
        pl.semaphore_signal(barrier, inc=1, device_id=peer, device_id_type=MESH)
    up_peer, down_peer = {"slab": slab + 2}, {"slab": slab - 2}
    near = [
        (here > 0, before_peer), (here < count - 1, after_peer),
        (z > 0, down_peer), (z < nz - 1, up_peer),
    ]
    greeted = 2
    for there, peer in near:
        @pl.when(there)
        def _():
            pl.semaphore_signal(barrier, inc=1, device_id=peer, device_id_type=MESH)

        greeted = greeted + there.astype(jnp.int32)

    def tell(which, peer):
        pl.semaphore_signal(told.at[which], inc=1, device_id=peer, device_id_type=MESH)

    def tell_first():
        if nz > 2:
            pl.when(z == 1)(lambda: tell(0, up_peer))
            pl.when(z == nz - 2)(lambda: tell(1, down_peer))

    def tell_on():
        @pl.when((z >= 2) & (z <= nz - 2))
        def _():
            pl.semaphore_wait(told.at[0], 1)
            tell(0, up_peer)

        @pl.when((z >= 1) & (z <= nz - 3))
        def _():
            pl.semaphore_wait(told.at[1], 1)
            tell(1, down_peer)

    def tell_last():
        if nz > 2:
            pl.when(z == nz - 1)(lambda: pl.semaphore_wait(told.at[0], 1))
            pl.when(z == 0)(lambda: pl.semaphore_wait(told.at[1], 1))
        tell(2, x_peer)

    loads = [
        pltpu.make_async_copy(basis, ext.at[pl.ds(layer, rows)], load_sem.at[0]),
        pltpu.make_async_copy(stiff, stiff_v, load_sem.at[1]),
        pltpu.make_async_copy(soft, soft_v, load_sem.at[2]),
        pltpu.make_async_copy(under, mask_v, load_sem.at[3]),
    ]
    for load in loads:
        load.start()

    def remote(src, dst, send, recv, peer):
        return pltpu.make_async_remote_copy(
            src_ref=src, dst_ref=dst, send_sem=send, recv_sem=recv,
            device_id=peer, device_id_type=MESH,
        )

    first_out = remote(
        basis.at[pl.ds(0, layer)], ext.at[pl.ds(layer + rows, layer)],
        halo_s.at[0], halo_r.at[0], before_peer,
    )
    last_out = remote(
        basis.at[pl.ds(rows - layer, layer)], ext.at[pl.ds(0, layer)],
        halo_s.at[1], halo_r.at[1], after_peer,
    )
    lower_out = remote(
        stiff.at[cells - 1, pl.ds(layer, layer)], stiff_p,
        halo_s.at[2], halo_r.at[2], after_peer,
    )

    def halo_out():
        @pl.when(here > 0)
        def _():
            first_out.start()

        @pl.when(here < count - 1)
        def _():
            last_out.start()
            lower_out.start()

    def halo_in():
        @pl.when(here > 0)
        def _():
            last_out.wait_recv()
            lower_out.wait_recv()

        @pl.when(here == 0)
        def _():
            ext[pl.ds(0, layer), :] = jnp.zeros((layer, width), BF16)
            stiff_p[...] = jnp.zeros(stiff_p.shape, BF16)

        @pl.when(here < count - 1)
        def _():
            first_out.wait_recv()

        @pl.when(here == count - 1)
        def _():
            ext[pl.ds(layer + rows, layer), :] = jnp.zeros((layer, width), BF16)

    def across(left, right):
        return lax.dot_general(
            left, right, (((0,), (0,)), ((), ())), preferred_element_type=F32
        )

    def stiff_inner(j):
        cols = pl.ds(j * chunk, chunk)
        carry = None
        for c in range(cells - 1):
            at = c * layer
            prod = jnp.dot(
                stiff_v[c], ext[pl.ds(at + layer, 2 * layer), cols], preferred_element_type=F32
            )
            if c == 0:
                held[0, :, cols] = prod[:layer]
            else:
                acted[pl.ds(at, layer), cols] = (prod[:layer] + carry).astype(BF16)
            carry = prod[layer:]
        held[1, :, cols] = carry

    def soft_chunk(j):
        cols = pl.ds(j * chunk, chunk)
        for c in range(cells):
            at = c * layer
            masked = soft_v[c] * mask_v[c].astype(F32).astype(BF16)
            prod = jnp.dot(
                masked, ext[pl.ds(at + layer, layer), cols], preferred_element_type=F32
            )
            softened[pl.ds(at, layer), cols] = prod.astype(BF16)

    kc = [remote(k_core_s.at[j, 1 - core], k_core_r.at[j], kc_s.at[j], kc_r.at[j], core_peer)
          for j in range(chunks)]
    kp = [[remote(k_s.at[j, p], k_r.at[j, p], kp_s.at[j, p], kp_r.at[j, p], peer)
           for p, peer in enumerate(chip_peers)] for j in range(chunks)]
    ec = [remote(e_core_s.at[j, 1 - core], e_core_r.at[j], ec_s.at[j], ec_r.at[j], core_peer)
          for j in range(chunks)]
    ex = [remote(e_x_s.at[j], e_x_r.at[j], ex_s.at[j], ex_r.at[j], x_peer) for j in range(chunks)]

    def k_blocks():
        for c in range(2):
            for xx in range(2):
                for zz in range(nz):
                    yield c, xx, zz, ((zz * 2 + xx) * 2 + c) * k_rows

    def k_inner(j):
        part = across(
            ext[pl.ds(2 * layer, rows - 2 * layer), :],
            acted[pl.ds(layer, rows - 2 * layer), pl.ds(j * chunk, chunk)],
        )
        for c, xx, zz, at in k_blocks():
            k_own[j, c, xx, zz] = part[at:at + k_rows]

    def k_start(j):
        cols = pl.ds(j * chunk, chunk)
        low = held[0, :, cols] + jnp.dot(
            stiff_p[...], ext[pl.ds(0, 2 * layer), cols], preferred_element_type=F32
        )
        high = held[1, :, cols] + jnp.dot(
            stiff_v[cells - 1, pl.ds(0, layer)], ext[pl.ds(rows, 2 * layer), cols],
            preferred_element_type=F32,
        )
        part = across(
            jnp.concatenate([ext[pl.ds(layer, layer), :], ext[pl.ds(rows, layer), :]], axis=0),
            jnp.concatenate([low.astype(BF16), high.astype(BF16)], axis=0),
        )
        for c, xx, zz, at in k_blocks():
            block = k_own[j, c, xx, zz] + part[at:at + k_rows]
            k_own[j, c, xx, zz] = block
            k_core_s[j, c, xx, zz] = block.astype(BF16)
        kc[j].start()

    def k_across(j):
        kc[j].wait_recv()
        for p, (zz, xx) in enumerate(places):
            k_s[j, p] = (k_own[j, core, xx, zz] + k_core_r[j, xx, zz].astype(F32)).astype(BF16)
            kp[j][p].start()

    def k_end(j):
        total = k_own[j, core, x, z] + k_core_r[j, x, z].astype(F32)
        for p in reversed(range(len(places))):
            kp[j][p].wait_recv()
            total = total + k_r[j, p].astype(F32)
        k_out[:, pl.ds(j * chunk, chunk)] = total

    def e_inner(j):
        part = across(ext[pl.ds(layer, rows), :], softened[:, pl.ds(j * chunk, chunk)])
        for c in range(2):
            for xx in range(2):
                at = (xx * 2 + c) * e_rows
                block = part[at:at + e_rows]
                e_own[j, c, xx] = block
                e_core_s[j, c, xx] = block.astype(BF16)

    def e_across(j):
        ec[j].wait_recv()
        e_x_s[j] = (e_own[j, core, 1 - x] + e_core_r[j, 1 - x].astype(F32)).astype(BF16)
        ex[j].start()

    def e_end(j):
        mine = e_own[j, core, x] + e_core_r[j, x].astype(F32)
        ex[j].wait_recv()
        e_out[:, pl.ds(j * chunk, chunk)] = mine + e_x_r[j].astype(F32)

    pl.semaphore_wait(barrier, greeted)
    halo_out()
    tell_first()
    for load in loads[:2]:
        load.wait()
    stiff_inner(0)
    k_inner(0)
    tell_on()
    stiff_inner(1)
    k_inner(1)
    tell_last()
    halo_in()
    k_start(0)
    k_start(1)
    for load in loads[2:]:
        load.wait()
    soft_chunk(0)
    pl.semaphore_wait(told.at[2], 1)
    k_across(0)
    k_across(1)
    e_inner(0)
    ec[0].start()
    soft_chunk(1)
    e_inner(1)
    ec[1].start()
    e_across(0)
    e_across(1)
    e_end(0)
    e_end(1)
    k_end(0)
    k_end(1)

    @pl.when(here > 0)
    def _():
        first_out.wait_send()

    @pl.when(here < count - 1)
    def _():
        last_out.wait_send()
        lower_out.wait_send()

    for j in range(chunks):
        kc[j].wait_send()
        for copy in kp[j]:
            copy.wait_send()
        ec[j].wait_send()
        ex[j].wait_send()


def hand_on(k_in, e_in, k_out, e_out, sem):
    copies = [
        pltpu.make_async_copy(e_in, e_out, sem.at[0]),
        pltpu.make_async_copy(k_in, k_out, sem.at[1]),
    ]
    for copy in copies:
        copy.start()
    for copy in copies:
        copy.wait()


def fused_body(basis, stiff, soft, under):
    cells, layer, width = basis.shape
    rows = cells * layer
    nz = lax.axis_size("slab") // 2
    chunk = 256
    chunks = width // chunk
    k_rows = width // (4 * nz)
    e_rows = width // 4
    others = 2 * nz - 1
    hbm = pl.BlockSpec(memory_space=pl.ANY)
    vmem = pl.BlockSpec(memory_space=pltpu.VMEM)
    dma = pltpu.SemaphoreType.DMA
    shapes = (
        jax.ShapeDtypeStruct((k_rows, width), F32),
        jax.ShapeDtypeStruct((e_rows, width), F32),
    )
    k_red, e_red = pl.pallas_call(
        functools.partial(fused_kernel, nz, cells, layer, width, chunk),
        out_shape=(pltpu.VMEM((k_rows, width), F32), pltpu.VMEM((e_rows, width), F32)),
        in_specs=[hbm] * 4,
        out_specs=(vmem, vmem),
        scratch_shapes=[
            pltpu.VMEM((rows + 2 * layer, width), BF16),
            pltpu.VMEM((cells, 2 * layer, 2 * layer), BF16),
            pltpu.VMEM((layer, 2 * layer), BF16),
            pltpu.VMEM((cells, layer, layer), BF16),
            pltpu.SMEM((cells,), jnp.int32),
            pltpu.VMEM((rows, width), BF16),
            pltpu.VMEM((rows, width), BF16),
            pltpu.VMEM((2, layer, width), F32),
            pltpu.VMEM((chunks, 2, 2, nz, k_rows, chunk), F32),
            pltpu.VMEM((chunks, 2, 2, nz, k_rows, chunk), BF16),
            pltpu.VMEM((chunks, 2, nz, k_rows, chunk), BF16),
            pltpu.VMEM((chunks, others, k_rows, chunk), BF16),
            pltpu.VMEM((chunks, others, k_rows, chunk), BF16),
            pltpu.VMEM((chunks, 2, 2, e_rows, chunk), F32),
            pltpu.VMEM((chunks, 2, 2, e_rows, chunk), BF16),
            pltpu.VMEM((chunks, 2, e_rows, chunk), BF16),
            pltpu.VMEM((chunks, e_rows, chunk), BF16),
            pltpu.VMEM((chunks, e_rows, chunk), BF16),
            dma((4,)), dma((3,)), dma((3,)),
            dma((chunks,)), dma((chunks,)),
            dma((chunks, others)), dma((chunks, others)),
            dma((chunks,)), dma((chunks,)), dma((chunks,)), dma((chunks,)),
            pltpu.SemaphoreType.REGULAR((3,)),
        ],
        compiler_params=pltpu.CompilerParams(
            collective_id=0, has_side_effects=True, vmem_limit_bytes=60 << 20
        ),
        name="fused",
    )(basis.reshape(rows, width), stiff, soft, under)
    return pl.pallas_call(
        hand_on,
        out_shape=shapes,
        in_specs=[vmem, vmem],
        out_specs=(hbm, hbm),
        scratch_shapes=[dma((2,))],
        compiler_params=pltpu.CompilerParams(vmem_limit_bytes=32 << 20),
        name="hand_on",
    )(k_red, e_red)


def solution(mesh):
    placed = (
        P(("groups", "slab", "cross"), None, None),
        P(("groups", "slab", "cross"), None, None),
        P(("groups", "slab", "cross"), None, None),
        P(("groups", "slab", "cross")),
    )

    def body(basis, stiff, soft, under):
        cells, layer, width = basis.shape
        members = mesh.shape["slab"] * mesh.shape["cross"]
        fits = (
            mesh.shape["cross"] == 2
            and mesh.shape["slab"] % 2 == 0
            and mesh.shape["slab"] >= 4
            and width == 512
            and layer == 64
            and cells % 4 == 0
            and (cells * layer) % 256 == 0
            and width // members >= 16
            and (width // members) % 16 == 0
        )
        return (fused_body if fits else plain_body)(basis, stiff, soft, under)

    return jax.shard_map(
        body,
        mesh=mesh,
        in_specs=placed,
        out_specs=(P(("groups", "slab", "cross"), None), P(("groups", "slab", "cross"), None)),
        check_vma=False,
    )
```

```python
import functools

import jax
import jax.numpy as jnp
from jax import lax
from jax.experimental import pallas as pl
from jax.experimental.pallas import tpu as pltpu
from jax.sharding import PartitionSpec as P

MESH = pl.DeviceIdType.MESH
BF16 = jnp.bfloat16
F32 = jnp.float32


def shifted(x, axis, by):
    length = lax.axis_size(axis)
    pairs = [(i, i + by) for i in range(length) if 0 <= i + by < length]
    return lax.ppermute(x, axis, pairs)


def partner(x, axis, bit):
    return lax.ppermute(x, axis, [(i, i ^ 1 << bit) for i in range(lax.axis_size(axis))])


def plain_body(basis, stiff, soft, under):
    cells, layer, width = basis.shape
    nextcell = shifted(basis[:1], ("slab", "cross"), -1)
    upper_cells = jnp.concatenate([basis[1:], nextcell], axis=0)
    pairs = jnp.concatenate([basis, upper_cells], axis=1)
    prod = jnp.einsum("cij,cjr->cir", stiff, pairs, preferred_element_type=jnp.float32)
    carry_in = shifted(prod[-1:, layer:], ("slab", "cross"), 1)
    action = prod[:, :layer] + jnp.concatenate([carry_in, prod[:-1, layer:]], axis=0)
    flat_basis = basis.reshape(cells * layer, width)
    flat_stiff = action.astype(jnp.bfloat16).reshape(cells * layer, width)
    k_reduced = lax.psum_scatter(
        lax.dot_general(
            flat_basis, flat_stiff, (((0,), (0,)), ((), ())), preferred_element_type=jnp.float32
        ),
        ("slab", "cross"),
        scatter_dimension=0,
        tiled=True,
    )
    masked = soft * under.astype(jnp.bfloat16)[:, None, None]
    soft_basis = jnp.einsum("cij,cjr->cir", masked, basis, preferred_element_type=jnp.float32)
    flat_soft = soft_basis.astype(jnp.bfloat16).reshape(cells * layer, width)
    partial_sum = lax.dot_general(
        flat_basis, flat_soft, (((0,), (0,)), ((), ())), preferred_element_type=jnp.float32
    )
    parity = lax.axis_index("slab") % 2
    halves = partial_sum.reshape(2, width // 2, width)
    mine = lax.dynamic_index_in_dim(halves, parity, 0, keepdims=False)
    other = lax.dynamic_index_in_dim(halves, 1 - parity, 0, keepdims=False)
    paired = mine + partner(other, "slab", 0)
    electrode_rows = lax.psum_scatter(paired, "cross", scatter_dimension=0, tiled=True)
    return (k_reduced, electrode_rows)


def fused_kernel(
    nz, cells, layer, width, chunk,
    basis, stiff, soft, under, k_out, e_out,
    ext, stiff_v, stiff_p, soft_v, mask_v, acted, softened, held,
    k_own, k_core_s, k_core_r, k_s, k_r,
    e_own, e_core_s, e_core_r, e_x_s, e_x_r,
    load_sem, halo_s, halo_r, kc_s, kc_r, kp_s, kp_r, ec_s, ec_r, ex_s, ex_r, told,
):
    slab = lax.axis_index("slab")
    core = lax.axis_index("cross")
    z, x = slab // 2, slab % 2
    here = slab * 2 + core
    count = nz * 4
    rows = cells * layer
    chunks = width // chunk
    k_rows = width // count
    e_rows = width // 4

    core_peer = {"cross": 1 - core}
    x_peer = {"slab": slab + 1 - 2 * x}
    turns = [nz // 2] + [d for d in range(1, nz) if d != nz // 2]
    places = [((z + d) % nz, (x + e) % 2) for e in (1, 0) for d in turns] + [(z, 1 - x)]
    chip_peers = [{"slab": zz * 2 + xx} for zz, xx in places]
    before = (here + count - 1) % count
    after = (here + 1) % count
    before_peer = {"slab": before // 2, "cross": before % 2}
    after_peer = {"slab": after // 2, "cross": after % 2}

    barrier = pltpu.get_barrier_semaphore()
    for peer in (core_peer, x_peer):
        pl.semaphore_signal(barrier, inc=1, device_id=peer, device_id_type=MESH)
    up_peer, down_peer = {"slab": slab + 2}, {"slab": slab - 2}
    near = [
        (here > 0, before_peer), (here < count - 1, after_peer),
        (z > 0, down_peer), (z < nz - 1, up_peer),
    ]
    greeted = 2
    for there, peer in near:
        @pl.when(there)
        def _():
            pl.semaphore_signal(barrier, inc=1, device_id=peer, device_id_type=MESH)

        greeted = greeted + there.astype(jnp.int32)

    def tell(which, peer):
        pl.semaphore_signal(told.at[which], inc=1, device_id=peer, device_id_type=MESH)

    def tell_first():
        if nz > 2:
            pl.when(z == 1)(lambda: tell(0, up_peer))
            pl.when(z == nz - 2)(lambda: tell(1, down_peer))

    def tell_on():
        @pl.when((z >= 2) & (z <= nz - 2))
        def _():
            pl.semaphore_wait(told.at[0], 1)
            tell(0, up_peer)

        @pl.when((z >= 1) & (z <= nz - 3))
        def _():
            pl.semaphore_wait(told.at[1], 1)
            tell(1, down_peer)

    def tell_last():
        if nz > 2:
            pl.when(z == nz - 1)(lambda: pl.semaphore_wait(told.at[0], 1))
            pl.when(z == 0)(lambda: pl.semaphore_wait(told.at[1], 1))
        tell(2, x_peer)

    loads = [
        pltpu.make_async_copy(basis, ext.at[pl.ds(layer, rows)], load_sem.at[0]),
        pltpu.make_async_copy(stiff, stiff_v, load_sem.at[1]),
        pltpu.make_async_copy(soft, soft_v, load_sem.at[2]),
        pltpu.make_async_copy(under, mask_v, load_sem.at[3]),
    ]
    for load in loads:
        load.start()

    def remote(src, dst, send, recv, peer):
        return pltpu.make_async_remote_copy(
            src_ref=src, dst_ref=dst, send_sem=send, recv_sem=recv,
            device_id=peer, device_id_type=MESH,
        )

    first_out = remote(
        basis.at[pl.ds(0, layer)], ext.at[pl.ds(layer + rows, layer)],
        halo_s.at[0], halo_r.at[0], before_peer,
    )
    last_out = remote(
        basis.at[pl.ds(rows - layer, layer)], ext.at[pl.ds(0, layer)],
        halo_s.at[1], halo_r.at[1], after_peer,
    )
    lower_out = remote(
        stiff.at[cells - 1, pl.ds(layer, layer)], stiff_p,
        halo_s.at[2], halo_r.at[2], after_peer,
    )

    def halo_out():
        @pl.when(here > 0)
        def _():
            first_out.start()

        @pl.when(here < count - 1)
        def _():
            last_out.start()
            lower_out.start()

    def halo_in():
        @pl.when(here > 0)
        def _():
            last_out.wait_recv()
            lower_out.wait_recv()

        @pl.when(here == 0)
        def _():
            ext[pl.ds(0, layer), :] = jnp.zeros((layer, width), BF16)
            stiff_p[...] = jnp.zeros(stiff_p.shape, BF16)

        @pl.when(here < count - 1)
        def _():
            first_out.wait_recv()

        @pl.when(here == count - 1)
        def _():
            ext[pl.ds(layer + rows, layer), :] = jnp.zeros((layer, width), BF16)

    def across(left, right):
        return lax.dot_general(
            left, right, (((0,), (0,)), ((), ())), preferred_element_type=F32
        )

    def stiff_inner(j):
        cols = pl.ds(j * chunk, chunk)
        carry = None
        for c in range(cells - 1):
            at = c * layer
            prod = jnp.dot(
                stiff_v[c], ext[pl.ds(at + layer, 2 * layer), cols], preferred_element_type=F32
            )
            if c == 0:
                held[0, :, cols] = prod[:layer]
            else:
                acted[pl.ds(at, layer), cols] = (prod[:layer] + carry).astype(BF16)
            carry = prod[layer:]
        held[1, :, cols] = carry

    def soft_chunk(j):
        cols = pl.ds(j * chunk, chunk)
        for c in range(cells):
            at = c * layer
            masked = soft_v[c] * mask_v[c].astype(F32).astype(BF16)
            prod = jnp.dot(
                masked, ext[pl.ds(at + layer, layer), cols], preferred_element_type=F32
            )
            softened[pl.ds(at, layer), cols] = prod.astype(BF16)

    kc = [remote(k_core_s.at[j, 1 - core], k_core_r.at[j], kc_s.at[j], kc_r.at[j], core_peer)
          for j in range(chunks)]
    kp = [[remote(k_s.at[j, p], k_r.at[j, p], kp_s.at[j, p], kp_r.at[j, p], peer)
           for p, peer in enumerate(chip_peers)] for j in range(chunks)]
    ec = [remote(e_core_s.at[j, 1 - core], e_core_r.at[j], ec_s.at[j], ec_r.at[j], core_peer)
          for j in range(chunks)]
    ex = [remote(e_x_s.at[j], e_x_r.at[j], ex_s.at[j], ex_r.at[j], x_peer) for j in range(chunks)]

    def k_blocks():
        for c in range(2):
            for xx in range(2):
                for zz in range(nz):
                    yield c, xx, zz, ((zz * 2 + xx) * 2 + c) * k_rows

    def k_inner(j):
        part = across(
            ext[pl.ds(2 * layer, rows - 2 * layer), :],
            acted[pl.ds(layer, rows - 2 * layer), pl.ds(j * chunk, chunk)],
        )
        for c, xx, zz, at in k_blocks():
            k_own[j, c, xx, zz] = part[at:at + k_rows]

    def k_start(j):
        cols = pl.ds(j * chunk, chunk)
        low = held[0, :, cols] + jnp.dot(
            stiff_p[...], ext[pl.ds(0, 2 * layer), cols], preferred_element_type=F32
        )
        high = held[1, :, cols] + jnp.dot(
            stiff_v[cells - 1, pl.ds(0, layer)], ext[pl.ds(rows, 2 * layer), cols],
            preferred_element_type=F32,
        )
        part = across(
            jnp.concatenate([ext[pl.ds(layer, layer), :], ext[pl.ds(rows, layer), :]], axis=0),
            jnp.concatenate([low.astype(BF16), high.astype(BF16)], axis=0),
        )
        for c, xx, zz, at in k_blocks():
            block = k_own[j, c, xx, zz] + part[at:at + k_rows]
            k_own[j, c, xx, zz] = block
            k_core_s[j, c, xx, zz] = block.astype(BF16)
        kc[j].start()

    def k_across(j):
        kc[j].wait_recv()
        for p, (zz, xx) in enumerate(places):
            k_s[j, p] = (k_own[j, core, xx, zz] + k_core_r[j, xx, zz].astype(F32)).astype(BF16)
            kp[j][p].start()

    def k_end(j):
        total = k_own[j, core, x, z] + k_core_r[j, x, z].astype(F32)
        for p in reversed(range(len(places))):
            kp[j][p].wait_recv()
            total = total + k_r[j, p].astype(F32)
        k_out[:, pl.ds(j * chunk, chunk)] = total

    def e_inner(j):
        part = across(ext[pl.ds(layer, rows), :], softened[:, pl.ds(j * chunk, chunk)])
        for c in range(2):
            for xx in range(2):
                at = (xx * 2 + c) * e_rows
                block = part[at:at + e_rows]
                e_own[j, c, xx] = block
                e_core_s[j, c, xx] = block.astype(BF16)

    def e_across(j):
        ec[j].wait_recv()
        e_x_s[j] = (e_own[j, core, 1 - x] + e_core_r[j, 1 - x].astype(F32)).astype(BF16)
        ex[j].start()

    def e_end(j):
        mine = e_own[j, core, x] + e_core_r[j, x].astype(F32)
        ex[j].wait_recv()
        e_out[:, pl.ds(j * chunk, chunk)] = mine + e_x_r[j].astype(F32)

    pl.semaphore_wait(barrier, greeted)
    halo_out()
    tell_first()
    for load in loads[:2]:
        load.wait()
    stiff_inner(0)
    k_inner(0)
    tell_on()
    stiff_inner(1)
    k_inner(1)
    tell_last()
    halo_in()
    k_start(0)
    k_start(1)
    for load in loads[2:]:
        load.wait()
    soft_chunk(0)
    pl.semaphore_wait(told.at[2], 1)
    k_across(0)
    k_across(1)
    e_inner(0)
    ec[0].start()
    soft_chunk(1)
    e_inner(1)
    ec[1].start()
    e_across(0)
    e_across(1)
    e_end(0)
    e_end(1)
    k_end(0)
    k_end(1)

    @pl.when(here > 0)
    def _():
        first_out.wait_send()

    @pl.when(here < count - 1)
    def _():
        last_out.wait_send()
        lower_out.wait_send()

    for j in range(chunks):
        kc[j].wait_send()
        for copy in kp[j]:
            copy.wait_send()
        ec[j].wait_send()
        ex[j].wait_send()


def hand_on(k_in, e_in, k_out, e_out, sem):
    copies = [
        pltpu.make_async_copy(e_in, e_out, sem.at[0]),
        pltpu.make_async_copy(k_in, k_out, sem.at[1]),
    ]
    for copy in copies:
        copy.start()
    for copy in copies:
        copy.wait()


def fused_body(basis, stiff, soft, under):
    cells, layer, width = basis.shape
    rows = cells * layer
    nz = lax.axis_size("slab") // 2
    chunk = 256
    chunks = width // chunk
    k_rows = width // (4 * nz)
    e_rows = width // 4
    others = 2 * nz - 1
    hbm = pl.BlockSpec(memory_space=pl.ANY)
    vmem = pl.BlockSpec(memory_space=pltpu.VMEM)
    dma = pltpu.SemaphoreType.DMA
    shapes = (
        jax.ShapeDtypeStruct((k_rows, width), F32),
        jax.ShapeDtypeStruct((e_rows, width), F32),
    )
    k_red, e_red = pl.pallas_call(
        functools.partial(fused_kernel, nz, cells, layer, width, chunk),
        out_shape=(pltpu.VMEM((k_rows, width), F32), pltpu.VMEM((e_rows, width), F32)),
        in_specs=[hbm] * 4,
        out_specs=(vmem, vmem),
        scratch_shapes=[
            pltpu.VMEM((rows + 2 * layer, width), BF16),
            pltpu.VMEM((cells, 2 * layer, 2 * layer), BF16),
            pltpu.VMEM((layer, 2 * layer), BF16),
            pltpu.VMEM((cells, layer, layer), BF16),
            pltpu.SMEM((cells,), jnp.int32),
            pltpu.VMEM((rows, width), BF16),
            pltpu.VMEM((rows, width), BF16),
            pltpu.VMEM((2, layer, width), F32),
            pltpu.VMEM((chunks, 2, 2, nz, k_rows, chunk), F32),
            pltpu.VMEM((chunks, 2, 2, nz, k_rows, chunk), BF16),
            pltpu.VMEM((chunks, 2, nz, k_rows, chunk), BF16),
            pltpu.VMEM((chunks, others, k_rows, chunk), BF16),
            pltpu.VMEM((chunks, others, k_rows, chunk), BF16),
            pltpu.VMEM((chunks, 2, 2, e_rows, chunk), F32),
            pltpu.VMEM((chunks, 2, 2, e_rows, chunk), BF16),
            pltpu.VMEM((chunks, 2, e_rows, chunk), BF16),
            pltpu.VMEM((chunks, e_rows, chunk), BF16),
            pltpu.VMEM((chunks, e_rows, chunk), BF16),
            dma((4,)), dma((3,)), dma((3,)),
            dma((chunks,)), dma((chunks,)),
            dma((chunks, others)), dma((chunks, others)),
            dma((chunks,)), dma((chunks,)), dma((chunks,)), dma((chunks,)),
            pltpu.SemaphoreType.REGULAR((3,)),
        ],
        compiler_params=pltpu.CompilerParams(
            collective_id=0, has_side_effects=True, vmem_limit_bytes=60 << 20
        ),
        name="fused",
    )(basis.reshape(rows, width), stiff, soft, under)
    return pl.pallas_call(
        hand_on,
        out_shape=shapes,
        in_specs=[vmem, vmem],
        out_specs=(hbm, hbm),
        scratch_shapes=[dma((2,))],
        compiler_params=pltpu.CompilerParams(vmem_limit_bytes=32 << 20),
        name="hand_on",
    )(k_red, e_red)


def solution(mesh):
    placed = (
        P(("groups", "slab", "cross"), None, None),
        P(("groups", "slab", "cross"), None, None),
        P(("groups", "slab", "cross"), None, None),
        P(("groups", "slab", "cross")),
    )

    def body(basis, stiff, soft, under):
        cells, layer, width = basis.shape
        members = mesh.shape["slab"] * mesh.shape["cross"]
        fits = (
            mesh.shape["cross"] == 2
            and mesh.shape["slab"] % 2 == 0
            and mesh.shape["slab"] >= 4
            and width == 512
            and layer == 64
            and cells % 4 == 0
            and (cells * layer) % 256 == 0
            and width // members >= 16
            and (width // members) % 16 == 0
        )
        return (fused_body if fits else plain_body)(basis, stiff, soft, under)

    return jax.shard_map(
        body,
        mesh=mesh,
        in_specs=placed,
        out_specs=(P(("groups", "slab", "cross"), None), P(("groups", "slab", "cross"), None)),
        check_vma=False,
    )
```
